256 devices in a mesh: dp: 8 (over y, core), lang: 32 (over x, z).
Axes of the slice: x: 4, y: 4, z: 8, core: 2. Of those that a mesh axis runs over, the one named last changes fastest.
Arguments:
- inputs: bfloat16 [32768, 2048], P(('dp', 'lang')), may hold values from -6 to 6
- grad_out: bfloat16 [32768, 2048], P(('dp', 'lang')), may hold values from -6 to 6
- lang_ids: int32 [32768], P(('dp', 'lang')), may hold values from 0 to 199, as said below
- lang_block: int32 [200], replicated, may hold values from 0 to 31, as said below
- block_owner: int32 [32], replicated, may hold values from 0 to 31, each once
- w_in: bfloat16 [32, 4096, 2048], P('lang', 'dp'), may hold values from -0.125 to 0.125
- w_out: bfloat16 [32, 4096, 2048], P('lang', 'dp'), may hold values from -0.09375 to 0.09375
Outputs:
- grad_in: bfloat16 [32768, 2048], P(('dp', 'lang'))
- grad_w_in: bfloat16 [32, 4096, 2048], P('lang', 'dp')
- grad_w_out: bfloat16 [32, 4096, 2048], P('lang', 'dp')
The draws below stay inside these ranges and needn't reach their ends.
Inputs may be any that keep to these rules, and one draw needn't show every extreme that they name: `lang_ids`: through lang_block, the 128 rows of one device name any one block at most 5 times; in every draw one block is named exactly 5 times by the rows of every device. `lang_block`: every block has at least one language. A permutation: block b's weights and gradients sit at index block_owner[b] of the block dimension.
All inputs are finite; a program needn't handle non-finite values.
Results may differ from the reference program's by a relative error of at most 0.019.
Values may be sent and summed in bfloat16 or wider, within the bound.
A program may use at most 128 MiB of HBM per device.

```python
import math
import jax
import jax.numpy as jnp
from jax import lax

D = 2048
FF = 4096
NLANGS = 200
TOK_DEV = 128
BLOCKS = 32
CAP = 5
TOKENS = 32768
N_DP = 8
N_LANG = 32


def route_tables(key):
    base_key = jax.random.fold_in(key, 7)
    k_order, k_popular, k_hot, k_noise, k_shuffle, k_pick = jax.random.split(base_key, 6)
    devices_all = TOKENS // TOK_DEV
    slots_all = BLOCKS * CAP
    lang_order = jax.random.permutation(k_order, NLANGS).astype(jnp.int32)
    lang_table = jnp.zeros((NLANGS,), jnp.int32).at[lang_order].set(jnp.arange(NLANGS, dtype=jnp.int32) % BLOCKS)
    popularity = jax.random.randint(k_popular, (BLOCKS,), 0, 3)
    hot_block = jax.random.randint(k_hot, (), 0, BLOCKS)
    pair_block = jnp.arange(slots_all, dtype=jnp.int32) // CAP
    base_score = popularity[pair_block] * 4096 + jnp.where(pair_block == hot_block, 16384, 0)
    row_noise = jax.random.randint(k_noise, (devices_all, slots_all), 0, 4096)
    slot_score = (base_score[None, :] + row_noise) * slots_all + jnp.arange(slots_all, dtype=jnp.int32)[None, :]
    chosen = jnp.argsort(-slot_score, axis=1)[:, :TOK_DEV].astype(jnp.int32)
    chosen_block = chosen // CAP
    shuffle_score = jax.random.randint(k_shuffle, (devices_all, TOK_DEV), 0, 65536) * TOK_DEV + jnp.arange(TOK_DEV, dtype=jnp.int32)[None, :]
    row_order = jnp.argsort(shuffle_score, axis=1)
    row_block = jnp.take_along_axis(chosen_block, row_order, axis=1).reshape(-1)
    per_block = (NLANGS - row_block + BLOCKS - 1) // BLOCKS
    lang_pick = jax.random.randint(k_pick, (TOKENS,), 0, 1 << 20) % per_block
    row_langs = lang_order[row_block + BLOCKS * lang_pick]
    return (lang_table, row_langs.astype(jnp.int32))


def draw_lang_ids(key, part):
    return route_tables(key)[1]


def draw_lang_block(key, part):
    return route_tables(key)[0]


def block_levels(stream_key, dims, cuts, smallest, top_value):
    def one(dim, shards_of):
        draws = jax.random.uniform(jax.random.fold_in(jax.random.fold_in(stream_key, 6), dim), (shards_of,), jnp.float32, smallest / len(cuts), top_value / len(cuts))
        return jnp.repeat(jnp.exp(draws), dims[dim] // shards_of).reshape((-1,) + (1,) * (len(dims) - dim - 1))

    level = one(*cuts[0])
    for cut in cuts[1:]:
        level = level * one(*cut)
    return level


def centred(stream_key, extent, deviation, most, cuts=(), kind=jnp.bfloat16):
    entries = deviation * jax.random.normal(stream_key, extent, jnp.float32)
    if cuts:
        entries = entries * block_levels(stream_key, extent, cuts, -0.22, 0.18)
    return jnp.clip(entries, -most, most).astype(kind)


def setup_inputs(seed: int = 0) -> dict:
    keys = jax.random.split(jax.random.key(seed), 8)
    inputs = centred(keys[0], (TOKENS, D), 1.0, 6.0, ((0, 256),))
    grad_out = centred(keys[1], (TOKENS, D), 1.0, 6.0, ((0, 256),))
    lang_ids = draw_lang_ids(jax.random.fold_in(keys[7], 71), 0)
    lang_block = draw_lang_block(jax.random.fold_in(keys[7], 71), 0)
    block_owner = jax.random.permutation(keys[4], BLOCKS).astype(jnp.int32)
    w_in = centred(keys[5], (BLOCKS, FF, D), D ** -0.5, 0.125, ((0, 32), (1, 8)))
    w_out = centred(keys[6], (BLOCKS, FF, D), FF ** -0.5, 0.09375, ((0, 32), (1, 8)))
    return dict(inputs=inputs, grad_out=grad_out, lang_ids=lang_ids, lang_block=lang_block, block_owner=block_owner, w_in=w_in, w_out=w_out)


gelu_scale = math.sqrt(2.0 / math.pi)

def gelu_parts(pre_act):
    tanh_arg = gelu_scale * (pre_act + 0.044715 * pre_act * pre_act * pre_act)
    tangent = jnp.tanh(tanh_arg)
    gelu_value = 0.5 * pre_act * (1.0 + tangent)
    gelu_slope = 0.5 * (1.0 + tangent) + 0.5 * pre_act * (1.0 - tangent * tangent) * gelu_scale * (1.0 + 3.0 * 0.044715 * pre_act * pre_act)
    return (gelu_value, gelu_slope)

def reference(inputs, grad_out, lang_ids, lang_block, block_owner, w_in, w_out):
    holder = block_owner[lang_block[lang_ids]]
    row_limit = N_DP * N_LANG * CAP
    ff_part = FF // N_DP

    def one_holder(holder_index):
        picked = jnp.nonzero(holder == holder_index, size=row_limit, fill_value=TOKENS)[0].astype(jnp.int32)
        rows_x = jnp.take(inputs, picked, axis=0, mode='fill', fill_value=0)
        rows_g = jnp.take(grad_out, picked, axis=0, mode='fill', fill_value=0)
        w_first = w_in[holder_index]
        w_second = w_out[holder_index]
        pre_act = jnp.dot(rows_x, w_first.T, preferred_element_type=jnp.float32)
        gelu_value, gelu_slope = gelu_parts(pre_act)
        activated = gelu_value.astype(jnp.bfloat16)
        back_grad = jnp.dot(rows_g, w_second.T, preferred_element_type=jnp.float32)
        pre_grad = (back_grad * gelu_slope).astype(jnp.bfloat16)
        g_out = jnp.dot(activated.T, rows_g, preferred_element_type=jnp.float32).astype(jnp.bfloat16)
        g_in = jnp.dot(pre_grad.T, rows_x, preferred_element_type=jnp.float32).astype(jnp.bfloat16)
        grad_split = pre_grad.astype(jnp.float32).reshape(row_limit, N_DP, ff_part)
        weight_split = w_first.astype(jnp.float32).reshape(N_DP, ff_part, D)
        dx_part = jnp.einsum('rkf,kfd->krd', grad_split, weight_split).astype(jnp.bfloat16)
        rows_dx = lax.optimization_barrier(jnp.sum(dx_part.astype(jnp.float32), axis=0)).astype(jnp.bfloat16)
        return (g_in, g_out, rows_dx, picked)
    g_in, g_out, rows_dx, picked = lax.map(one_holder, jnp.arange(BLOCKS, dtype=jnp.int32))
    grad_in = jnp.zeros((TOKENS, D), jnp.bfloat16).at[picked.reshape(-1)].set(rows_dx.reshape(-1, D), mode='drop')
    return (grad_in, g_in, g_out)
```

```python
import math

import jax
import jax.numpy as jnp
from jax import lax
from jax.sharding import PartitionSpec as P

gelu_scale = math.sqrt(2.0 / math.pi)
CAP = 5


def gelu_parts(pre_act):
    tanh_arg = gelu_scale * (pre_act + 0.044715 * pre_act * pre_act * pre_act)
    tangent = jnp.tanh(tanh_arg)
    gelu_value = 0.5 * pre_act * (1.0 + tangent)
    gelu_slope = 0.5 * (1.0 + tangent) + 0.5 * pre_act * (1.0 - tangent * tangent) * gelu_scale * (
        1.0 + 3.0 * 0.044715 * pre_act * pre_act
    )
    return (gelu_value, gelu_slope)


def local_grads(rows_x, rows_g, w_first, w_second):
    pre_act = jnp.dot(rows_x, w_first.T, preferred_element_type=jnp.float32)
    gelu_value, gelu_slope = gelu_parts(pre_act)
    activated = gelu_value.astype(jnp.bfloat16)
    back_grad = jnp.dot(rows_g, w_second.T, preferred_element_type=jnp.float32)
    pre_grad = (back_grad * gelu_slope).astype(jnp.bfloat16)
    g_out = jnp.dot(activated.T, rows_g, preferred_element_type=jnp.float32).astype(jnp.bfloat16)
    g_in = jnp.dot(pre_grad.T, rows_x, preferred_element_type=jnp.float32).astype(jnp.bfloat16)
    return (pre_grad, g_in, g_out)


def slots_of(lang_ids, lang_block, block_owner):
    rows = lang_ids.shape[0]
    holder_of_lang = jnp.sum(
        jnp.where(lang_block[:, None] == jnp.arange(block_owner.shape[0])[None, :], block_owner[None, :], 0), axis=1
    )
    holder = jnp.sum(
        jnp.where(lang_ids[:, None] == jnp.arange(lang_block.shape[0])[None, :], holder_of_lang[None, :], 0), axis=1
    )
    row = jnp.arange(rows)
    earlier = jnp.sum(((holder[:, None] == holder[None, :]) & (row[None, :] < row[:, None])).astype(jnp.int32), axis=1)
    return holder * CAP + earlier


def body(inputs, grad_out, lang_ids, lang_block, block_owner, w_in, w_out):
    feat = inputs.shape[1]
    n_lang = lax.axis_size("lang")
    slots = n_lang * CAP
    position = slots_of(lang_ids, lang_block, block_owner)
    onehot = (position[None, :] == jnp.arange(slots)[:, None]).astype(jnp.bfloat16)
    packed = jnp.concatenate([inputs, grad_out], axis=1)
    outgoing = jnp.dot(onehot, packed, preferred_element_type=jnp.float32).astype(jnp.bfloat16)
    outgoing = outgoing.reshape(n_lang, CAP * 2 * feat // 128, 128)
    arrived = lax.all_to_all(outgoing, "lang", split_axis=0, concat_axis=0, tiled=True)
    arrived = arrived.reshape(slots, 2 * feat)
    gathered = lax.all_gather(arrived, "dp", axis=0, tiled=True)
    pre_grad, g_in, g_out = local_grads(gathered[:, :feat], gathered[:, feat:], w_in[0], w_out[0])
    partial_dx = jnp.dot(pre_grad, w_in[0], preferred_element_type=jnp.float32).astype(jnp.bfloat16)
    summed = lax.psum_scatter(partial_dx, "dp", scatter_dimension=0, tiled=True)
    back = summed.reshape(n_lang, CAP * feat // 128, 128)
    returned = lax.all_to_all(back, "lang", split_axis=0, concat_axis=0, tiled=True)
    returned = returned.reshape(slots, feat)
    grad_in = jnp.dot(onehot.T, returned, preferred_element_type=jnp.float32).astype(jnp.bfloat16)
    return (grad_in, g_in[None], g_out[None])


def solution(mesh):
    in_specs = (
        P(("dp", "lang"), None),
        P(("dp", "lang"), None),
        P(("dp", "lang")),
        P(),
        P(),
        P("lang", "dp", None),
        P("lang", "dp", None),
    )
    out_specs = (P(("dp", "lang"), None), P("lang", "dp", None), P("lang", "dp", None))
    return jax.shard_map(body, mesh=mesh, in_specs=in_specs, out_specs=out_specs, check_vma=False)
```

```python
import functools
import math

import jax
import jax.numpy as jnp
from jax import lax
from jax.experimental import pallas as pl
from jax.experimental.pallas import tpu as pltpu
from jax.sharding import PartitionSpec as P

gelu_scale = math.sqrt(2.0 / math.pi)
CAP = 5
NX, NZ, NY = 4, 8, 4
LANE = 128
SUB = 16
TILES = 16
MESH = pl.DeviceIdType.MESH


def gelu_parts(pre_act):
    tanh_arg = gelu_scale * (pre_act + 0.044715 * pre_act * pre_act * pre_act)
    tangent = jnp.tanh(tanh_arg)
    gelu_value = 0.5 * pre_act * (1.0 + tangent)
    gelu_slope = 0.5 * (1.0 + tangent) + 0.5 * pre_act * (1.0 - tangent * tangent) * gelu_scale * (
        1.0 + 3.0 * 0.044715 * pre_act * pre_act
    )
    return (gelu_value, gelu_slope)


def slots_of(lang_ids, lang_block, block_owner):
    rows = lang_ids.shape[0]
    n_hold = block_owner.shape[0]
    holder_of_lang = jnp.sum(
        jnp.where(lang_block[:, None] == jnp.arange(n_hold)[None, :], block_owner[None, :], 0), axis=1
    )
    holder = jnp.sum(
        jnp.where(lang_ids[:, None] == jnp.arange(lang_block.shape[0])[None, :], holder_of_lang[None, :], 0), axis=1
    )
    row = jnp.arange(rows)
    earlier = jnp.sum(((holder[:, None] == holder[None, :]) & (row[None, :] < row[:, None])).astype(jnp.int32), axis=1)
    return earlier * n_hold + holder


def dot_nt(a, b):
    return lax.dot_general(a, b, (((1,), (1,)), ((), ())), preferred_element_type=jnp.float32)


def dot_nn(a, b):
    return lax.dot_general(a, b, (((1,), (0,)), ((), ())), preferred_element_type=jnp.float32)


def kernel(
    send0, w_in_hbm, w_out_hbm,
    back_ref, gw_in_ref, gw_out_ref,
    w_in, w_out, rx1, rx2, rows, act_t, pg_t, pg, tsend, trecv, own, r1s, r1r, r2s, r2r, fin, bz, bx,
    w_sem, x_send, x_recv, z_send, z_recv, a_send, f_send, h_send, y_recv, c_recv,
    t_send, t_recv, r1_send, r1_recv, r2_send, r2_recv, bz_send, bz_recv, bx_send, bx_recv,
):
    dp, lang = lax.axis_index("dp"), lax.axis_index("lang")
    y, k = dp // 2, dp % 2
    x, z = lang // NZ, lang % NZ
    y_up, y_down, y_far = (y + 1) % NY, (y + NY - 1) % NY, (y + 2) % NY
    up, down, twin = (y_up * 2 + k, lang), (y_down * 2 + k, lang), (y * 2 + 1 - k, lang)
    d_up, d_down, d_far = y_up * 2 + k, y_down * 2 + k, y_far * 2 + k
    x_peers = [(dp, ((x + i) % NX) * NZ + z) for i in range(1, NX)]
    z_peers = [(dp, x * NZ + (z + i) % NZ) for i in range(1, NZ)]

    def send(src, dst, s_sem, r_sem, to):
        pltpu.make_async_remote_copy(
            src_ref=src, dst_ref=dst, send_sem=s_sem, recv_sem=r_sem, device_id=to, device_id_type=MESH
        ).start()

    def take(ref, sem):
        pltpu.make_async_copy(ref, ref, sem).wait()

    w_copies = [
        pltpu.make_async_copy(w_in_hbm, w_in, w_sem.at[0]),
        pltpu.make_async_copy(w_out_hbm, w_out, w_sem.at[1]),
    ]
    for copy in w_copies:
        copy.start()

    barrier = pltpu.get_barrier_semaphore()
    peers = [up, down, twin, *x_peers, *z_peers]
    for peer in peers:
        pl.semaphore_signal(barrier, inc=1, device_id=peer, device_id_type=MESH)
    pl.semaphore_wait(barrier, len(peers))

    big_row = lax.broadcasted_iota(jnp.int32, (SUB * TILES, SUB * TILES), 0)
    big_col = lax.broadcasted_iota(jnp.int32, (SUB * TILES, SUB * TILES), 1)
    swap = jnp.where(big_col == (big_row % SUB) * TILES + big_row // SUB, 1.0, 0.0).astype(jnp.bfloat16)

    def start_x(c):
        pltpu.make_async_copy(send0.at[c, x], rx1.at[c, x], x_recv.at[c]).start()
        for i in range(1, NX):
            to = (x + i) % NX
            send(send0.at[c, to], rx1.at[c, x], x_send.at[c], x_recv.at[c], (dp, to * NZ + z))

    def start_z(c):
        take(rx1.at[c], x_recv.at[c])
        pltpu.make_async_copy(rx1.at[c, :, z], rx2.at[c, z], z_recv.at[c]).start()
        for i in (4, 3, 5, 2, 6, 1, 7):
            to = (z + i) % NZ
            send(rx1.at[c, :, to], rx2.at[c, z], z_send.at[c], z_recv.at[c], (dp, x * NZ + to))

    def start_gather(c):
        take(rx2.at[c], z_recv.at[c])
        for g in range(2):
            tiles = rx2[c, 4 * g : 4 * g + 4].reshape(SUB, 2 * TILES, LANE)
            tx = tiles[:, :TILES].reshape(SUB * TILES, LANE)
            tg = tiles[:, TILES:].reshape(SUB * TILES, LANE)
            both = dot_nn(swap, jnp.concatenate([tx, tg], axis=1)).astype(jnp.bfloat16)
            for j in range(TILES):
                part = both[j * SUB : (j + 1) * SUB]
                rows[c, dp, g * SUB : (g + 1) * SUB, j * LANE : (j + 1) * LANE] = part[:, :LANE]
                rows[c, dp, g * SUB : (g + 1) * SUB, (TILES + j) * LANE : (TILES + j + 1) * LANE] = part[:, LANE:]
        mine = rows.at[c, dp]
        send(mine, mine, a_send.at[c], y_recv.at[c, 0], up)
        send(mine, mine, a_send.at[c], y_recv.at[c, 1], down)
        send(mine, mine, a_send.at[c], c_recv.at[c, 0], twin)

    def forward(c):
        low, high = pl.ds(0, SUB), pl.ds(SUB, SUB)
        take(rows.at[c, d_down], y_recv.at[c, 0])
        block = rows.at[c, d_down, low]
        send(block, block, f_send.at[c], y_recv.at[c, 2], up)
        take(rows.at[c, d_up], y_recv.at[c, 1])
        block = rows.at[c, d_up, high]
        send(block, block, f_send.at[c], y_recv.at[c, 3], down)
        send(rows.at[c, d_down], rows.at[c, d_down], f_send.at[c], c_recv.at[c, 1], twin)
        send(rows.at[c, d_up], rows.at[c, d_up], f_send.at[c], c_recv.at[c, 2], twin)

    def forward_far(c):
        for i in range(2):
            block = rows.at[c, d_far, pl.ds(i * SUB, SUB)]
            take(block, y_recv.at[c, 2 + i])
            send(block, block, h_send.at[c], c_recv.at[c, 3], twin)

    def compute(c):
        t_own, t_down = y * 2 + 1 - k, y_down * 2 + 1 - k
        t_up, t_far = y_up * 2 + 1 - k, y_far * 2 + 1 - k
        for i, d in enumerate((t_own, t_down, t_up, t_far)):
            take(rows.at[c, d], c_recv.at[c, i])
        hid, feat = w_in.shape

        def hidden(f, _):
            at = pl.ds(pl.multiple_of(f * 256, 256), 256)
            x_rows = rows[c, :, :, :feat].reshape(2 * NY * 32, feat)
            g_rows = rows[c, :, :, feat:].reshape(2 * NY * 32, feat)
            value, slope = gelu_parts(dot_nt(x_rows, w_in[at, :]))
            pre_grad = (dot_nt(g_rows, w_out[at, :]) * slope).astype(jnp.bfloat16)
            act_t[c, at] = value.astype(jnp.bfloat16).T
            pg_t[c, at] = pre_grad.T
            pg[:, :, :, at] = pre_grad.reshape(NY, 2, 32, 256)
            return 0

        lax.fori_loop(0, hid // 256, hidden, 0)

        def away(f, _):
            at = pl.ds(pl.multiple_of(f * 512, 512), 512)
            part = dot_nn(pg[:, 1 - k].reshape(NY * 32, hid), w_in[:, at])
            tsend[c, :, :, at] = part.astype(jnp.bfloat16).reshape(NY, 32, 512)
            return 0

        lax.fori_loop(0, feat // 512, away, 0)
        send(tsend.at[c], trecv.at[c], t_send.at[c], t_recv.at[c], twin)

        def home(f, _):
            at = pl.ds(pl.multiple_of(f * 512, 512), 512)
            own[c % 4, :, :, at] = dot_nn(pg[:, k].reshape(NY * 32, hid), w_in[:, at]).reshape(NY, 32, 512)
            return 0

        lax.fori_loop(0, feat // 512, home, 0)

    def reduce_far(c):
        take(trecv.at[c], t_recv.at[c])
        o = c % 4
        for i in range(2):
            at = pl.ds(i * SUB, SUB)
            r1s[c, i] = (own[o, y_far, at] + trecv[c, y_far, at].astype(jnp.float32)).astype(jnp.bfloat16)
        send(r1s.at[c, 0], r1r.at[c, 0], r1_send.at[c], r1_recv.at[c, 0], up)
        send(r1s.at[c, 1], r1r.at[c, 1], r1_send.at[c], r1_recv.at[c, 1], down)

    def reduce_near(c):
        o = c % 4
        for i, (to, y_to, first) in enumerate(((up, y_up, 0), (down, y_down, SUB))):
            take(r1r.at[c, i], r1_recv.at[c, i])
            with_far, alone = pl.ds(first, SUB), pl.ds(SUB - first, SUB)
            total = own[o, y_to, with_far] + trecv[c, y_to, with_far].astype(jnp.float32)
            r2s[c, i, with_far] = (total + r1r[c, i].astype(jnp.float32)).astype(jnp.bfloat16)
            total = own[o, y_to, alone] + trecv[c, y_to, alone].astype(jnp.float32)
            r2s[c, i, alone] = total.astype(jnp.bfloat16)
            send(r2s.at[c, i], r2r.at[c, i], r2_send.at[c], r2_recv.at[c, i], to)
        own_sum = own[o, y] + trecv[c, y].astype(jnp.float32)
        own[o, y] = own_sum

    def reduce_last(c):
        o = c % 4
        for i in range(2):
            take(r2r.at[c, i], r2_recv.at[c, i])
        for g in range(2):
            at = pl.ds(g * SUB, SUB)
            total = own[o, y, at] + r2r[c, 0, at].astype(jnp.float32) + r2r[c, 1, at].astype(jnp.float32)
            total = total.astype(jnp.bfloat16)
            tall = jnp.concatenate([total[:, j * LANE : (j + 1) * LANE] for j in range(TILES)], axis=0)
            out = dot_nn(swap, tall).astype(jnp.bfloat16)
            fin[c, 4 * g : 4 * g + 4] = out.reshape(4, NX, TILES, LANE)
        pltpu.make_async_copy(fin.at[c, z], bz.at[c, z], bz_recv.at[c]).start()
        for i in (4, 3, 5, 2, 6, 1, 7):
            to = (z + i) % NZ
            send(fin.at[c, to], bz.at[c, z], bz_send.at[c], bz_recv.at[c], (dp, x * NZ + to))

    def start_back_x(c):
        take(bz.at[c], bz_recv.at[c])
        pltpu.make_async_copy(bz.at[c, :, x], bx.at[c, x], bx_recv.at[c]).start()
        for i in range(1, NX):
            to = (x + i) % NX
            send(bz.at[c, :, to], bx.at[c, x], bx_send.at[c], bx_recv.at[c], (dp, to * NZ + z))

    def finish(c):
        take(bx.at[c], bx_recv.at[c])
        for g in range(2):
            tall = bx[c, 2 * g : 2 * g + 2].reshape(SUB * TILES, LANE)
            out = dot_nn(swap, tall).astype(jnp.bfloat16)
            for j in range(TILES):
                back_ref[c, g * SUB : (g + 1) * SUB, j * LANE : (j + 1) * LANE] = out[j * SUB : (j + 1) * SUB]

    def weight_grads(f):
        feat = w_in.shape[1]
        at = pl.ds(pl.multiple_of(f * 256, 256), 256)
        at_g = pl.ds(pl.multiple_of(feat + f * 256, 256), 256)
        total_in = total_out = None
        for c in range(CAP):
            part_in = dot_nn(pg_t[c], rows[c, :, :, at].reshape(2 * NY * 32, 256))
            part_out = dot_nn(act_t[c], rows[c, :, :, at_g].reshape(2 * NY * 32, 256))
            total_in = part_in if c == 0 else total_in + part_in
            total_out = part_out if c == 0 else total_out + part_out
        gw_in_ref[:, at] = total_in.astype(jnp.bfloat16)
        gw_out_ref[:, at] = total_out.astype(jnp.bfloat16)

    start_x(0)
    start_x(1)

    stages = [
        (0, start_z),
        (1, start_gather),
        (2, forward),
        (4, reduce_far),
        (5, reduce_near),
        (6, reduce_last),
        (7, start_back_x),
        (8, finish),
        (2, forward_far),
        (3, compute),
    ]

    def tick(t, _):
        for offset, stage in stages[:1]:
            pl.when((t >= offset) & (t < offset + CAP))(functools.partial(stage, t - offset))
        pl.when(t + 2 < CAP)(lambda: start_x(t + 2))
        for offset, stage in stages[1:]:
            if stage is compute:
                @pl.when(t == 3)
                def _():
                    for copy in w_copies:
                        copy.wait()
            pl.when((t >= offset) & (t < offset + CAP))(functools.partial(stage, t - offset))

        @pl.when((t >= 8) & (t < 12))
        def _():
            lax.fori_loop(0, 2, lambda i, _: (weight_grads((t - 8) * 2 + i), 0)[1], 0)

        return 0

    lax.fori_loop(0, 8 + CAP, tick, 0)

    def drain(c, _):
        take(rx1.at[c, pl.ds(0, NX - 1)], x_send.at[c])
        take(rx2.at[c, pl.ds(0, NZ - 1)], z_send.at[c])
        take(rows.at[c, pl.ds(0, 3)], a_send.at[c])
        take(rows.at[c, pl.ds(0, 3)], f_send.at[c])
        take(rows.at[c, 0], h_send.at[c])
        take(tsend.at[c], t_send.at[c])
        take(r1s.at[c], r1_send.at[c])
        take(r2s.at[c], r2_send.at[c])
        take(fin.at[c, pl.ds(0, NZ - 1)], bz_send.at[c])
        take(bx.at[c, pl.ds(0, NX - 1)], bx_send.at[c])
        return 0

    lax.fori_loop(0, CAP, drain, 0)


def exchange_and_compute(outgoing, w_first, w_second):
    hid, feat = w_first.shape
    bf16, f32 = jnp.bfloat16, jnp.float32
    vmem = pl.BlockSpec(memory_space=pltpu.VMEM)
    dma = pltpu.SemaphoreType.DMA
    return pl.pallas_call(
        kernel,
        out_shape=(
            jax.ShapeDtypeStruct((CAP, NX * NZ, feat), bf16),
            jax.ShapeDtypeStruct((hid, feat), bf16),
            jax.ShapeDtypeStruct((hid, feat), bf16),
        ),
        in_specs=[vmem, pl.BlockSpec(memory_space=pl.ANY), pl.BlockSpec(memory_space=pl.ANY)],
        out_specs=(vmem, vmem, vmem),
        scratch_shapes=[
            pltpu.VMEM((hid, feat), bf16),
            pltpu.VMEM((hid, feat), bf16),
            pltpu.VMEM((CAP, NX, NZ, 2 * TILES, LANE), bf16),
            pltpu.VMEM((CAP, NZ, NX, 2 * TILES, LANE), bf16),
            pltpu.VMEM((CAP, 2 * NY, 32, 2 * feat), bf16),
            pltpu.VMEM((CAP, hid, 256), bf16),
            pltpu.VMEM((CAP, hid, 256), bf16),
            pltpu.VMEM((NY, 2, 32, hid), bf16),
            pltpu.VMEM((CAP, NY, 32, feat), bf16),
            pltpu.VMEM((CAP, NY, 32, feat), bf16),
            pltpu.VMEM((4, NY, 32, feat), f32),
            pltpu.VMEM((CAP, 2, SUB, feat), bf16),
            pltpu.VMEM((CAP, 2, SUB, feat), bf16),
            pltpu.VMEM((CAP, 2, 32, feat), bf16),
            pltpu.VMEM((CAP, 2, 32, feat), bf16),
            pltpu.VMEM((CAP, NZ, NX, TILES, LANE), bf16),
            pltpu.VMEM((CAP, NZ, NX, TILES, LANE), bf16),
            pltpu.VMEM((CAP, NX, NZ, TILES, LANE), bf16),
            dma((2,)),
            dma((CAP,)), dma((CAP,)), dma((CAP,)), dma((CAP,)),
            dma((CAP,)), dma((CAP,)), dma((CAP,)),
            dma((CAP, 4)), dma((CAP, 4)),
            dma((CAP,)), dma((CAP,)),
            dma((CAP,)), dma((CAP, 2)),
            dma((CAP,)), dma((CAP, 2)),
            dma((CAP,)), dma((CAP,)), dma((CAP,)), dma((CAP,)),
        ],
        compiler_params=pltpu.CompilerParams(
            collective_id=0, has_side_effects=True, vmem_limit_bytes=50 * 1024 * 1024
        ),
    )(outgoing, w_first, w_second)


def body(inputs, grad_out, lang_ids, lang_block, block_owner, w_in, w_out):
    feat = inputs.shape[1]
    slots = CAP * NX * NZ
    position = slots_of(lang_ids, lang_block, block_owner)
    onehot = (position[None, :] == jnp.arange(slots)[:, None]).astype(jnp.bfloat16)
    packed = jnp.concatenate([inputs, grad_out], axis=1)
    outgoing = jnp.dot(onehot, packed, preferred_element_type=jnp.float32).astype(jnp.bfloat16)
    outgoing = outgoing.reshape(CAP, NX, NZ, 2 * TILES, LANE)
    back, g_in, g_out = exchange_and_compute(outgoing, w_in[0], w_out[0])
    grad_in = jnp.dot(onehot.T, back.reshape(slots, feat), preferred_element_type=jnp.float32).astype(jnp.bfloat16)
    return (grad_in, g_in[None], g_out[None])


def solution(mesh):
    in_specs = (
        P(("dp", "lang"), None),
        P(("dp", "lang"), None),
        P(("dp", "lang")),
        P(),
        P(),
        P("lang", "dp", None),
        P("lang", "dp", None),
    )
    out_specs = (P(("dp", "lang"), None), P("lang", "dp", None), P("lang", "dp", None))
    return jax.shard_map(body, mesh=mesh, in_specs=in_specs, out_specs=out_specs, check_vma=False)
```

```python
import functools
import math

import jax
import jax.numpy as jnp
from jax import lax
from jax.experimental import pallas as pl
from jax.experimental.pallas import tpu as pltpu
from jax.sharding import PartitionSpec as P

gelu_scale = math.sqrt(2.0 / math.pi)
CAP = 5
NX, NZ, NY = 4, 8, 4
LANE = 128
SUB = 16
TILES = 16
MESH = pl.DeviceIdType.MESH


def gelu_parts(pre_act):
    tanh_arg = gelu_scale * (pre_act + 0.044715 * pre_act * pre_act * pre_act)
    tangent = jnp.tanh(tanh_arg)
    gelu_value = 0.5 * pre_act * (1.0 + tangent)
    gelu_slope = 0.5 * (1.0 + tangent) + 0.5 * pre_act * (1.0 - tangent * tangent) * gelu_scale * (
        1.0 + 3.0 * 0.044715 * pre_act * pre_act
    )
    return (gelu_value, gelu_slope)


def placement(route, swap_type):
    n_hold = NX * NZ

    def picks(shape, values):
        at = lax.broadcasted_iota(jnp.int32, shape, 0)
        return jnp.where(at == values, 1.0, 0.0).astype(swap_type)

    lang_of_row = picks((256, 128), route[:, 384:512])
    block_of_lang = dot_nn(picks((128, 256), route[:, 0:256]), lang_of_row).astype(swap_type)
    holder = dot_nn(picks((n_hold, 128), route[:, 256:384]), block_of_lang)
    row = lax.broadcasted_iota(jnp.int32, (128, 128), 0)
    later = lax.broadcasted_iota(jnp.int32, (128, 128), 1)
    before = jnp.where(row < later, 1.0, 0.0).astype(swap_type)
    earlier = dot_nn(holder.astype(swap_type), before)
    return [jnp.where(earlier == float(slot), holder, 0.0).astype(swap_type) for slot in range(CAP)]


def dot_nt(a, b):
    return lax.dot_general(a, b, (((1,), (1,)), ((), ())), preferred_element_type=jnp.float32)


def dot_nn(a, b):
    return lax.dot_general(a, b, (((1,), (0,)), ((), ())), preferred_element_type=jnp.float32)


def kernel(
    route_ref, x_hbm, g_hbm, w_in_hbm, w_out_hbm,
    grad_ref, gw_in_ref, gw_out_ref,
    x_ref, g_ref, w_in, w_out, place, total_ref, out_tiles, in_tiles, rows, act_t, pg_t, pg, slots, tsend, trecv, own, r1s, r1r, r2s, r2r, fin, back,
    w_sem, e_send, e_recv, a_send, f_send, h_send, y_recv, c_recv,
    t_send, t_recv, r1_send, r1_recv, r2_send, r2_recv, b_send, b_recv,
):
    dp, lang = lax.axis_index("dp"), lax.axis_index("lang")
    y, k = dp // 2, dp % 2
    n_hold = NX * NZ
    y_up, y_down, y_far = (y + 1) % NY, (y + NY - 1) % NY, (y + 2) % NY
    up, down, twin = (y_up * 2 + k, lang), (y_down * 2 + k, lang), (y * 2 + 1 - k, lang)
    d_up, d_down, d_far = y_up * 2 + k, y_down * 2 + k, y_far * 2 + k
    def send(src, dst, s_sem, r_sem, to):
        pltpu.make_async_remote_copy(
            src_ref=src, dst_ref=dst, send_sem=s_sem, recv_sem=r_sem, device_id=to, device_id_type=MESH
        ).start()

    def take(ref, sem):
        pltpu.make_async_copy(ref, ref, sem).wait()

    w_copies = [
        pltpu.make_async_copy(w_in_hbm, w_in, w_sem.at[0]),
        pltpu.make_async_copy(w_out_hbm, w_out, w_sem.at[1]),
    ]
    row_copies = [
        pltpu.make_async_copy(x_hbm, x_ref, w_sem.at[2]),
        pltpu.make_async_copy(g_hbm, g_ref, w_sem.at[3]),
    ]
    for copy in (*row_copies, *w_copies):
        copy.start()

    barrier = pltpu.get_barrier_semaphore()
    for peer in (up, down, twin):
        pl.semaphore_signal(barrier, inc=1, device_id=peer, device_id_type=MESH)

    def greet(i, _):
        pl.semaphore_signal(barrier, inc=1, device_id=(dp, (lang + i) % n_hold), device_id_type=MESH)
        return 0

    lax.fori_loop(1, n_hold, greet, 0)
    big_row = lax.broadcasted_iota(jnp.int32, (SUB * TILES, SUB * TILES), 0)
    big_col = lax.broadcasted_iota(jnp.int32, (SUB * TILES, SUB * TILES), 1)
    swap = jnp.where(big_col == (big_row % SUB) * TILES + big_row // SUB, 1.0, 0.0).astype(jnp.bfloat16)

    feat = w_in.shape[1]
    hid = w_in.shape[0]
    for slot, picked in enumerate(placement(route_ref[...], jnp.bfloat16)):
        place[slot] = picked

    def to_tiles(matrix, width):
        return jnp.concatenate([matrix[:, j * LANE : (j + 1) * LANE] for j in range(width)], axis=0)

    def dispatch(c):
        x_rows = dot_nn(place[c], x_ref[...]).astype(jnp.bfloat16)
        g_rows = dot_nn(place[c], g_ref[...]).astype(jnp.bfloat16)
        for g in range(2):
            at = slice(g * SUB, (g + 1) * SUB)
            both = jnp.concatenate([to_tiles(x_rows[at], TILES), to_tiles(g_rows[at], TILES)], axis=1)
            both = dot_nn(swap, both).astype(jnp.bfloat16)
            out_tiles[c, at, :TILES] = both[:, :LANE].reshape(SUB, TILES, LANE)
            out_tiles[c, at, TILES:] = both[:, LANE:].reshape(SUB, TILES, LANE)

    def start_exchange(c):
        pltpu.make_async_copy(out_tiles.at[c, lang], in_tiles.at[c, lang], e_recv.at[c]).start()

        def one(i, _):
            to = (lang + i) % n_hold
            send(out_tiles.at[c, to], in_tiles.at[c, lang], e_send.at[c], e_recv.at[c], (dp, to))
            return 0

        lax.fori_loop(1, n_hold, one, 0)

    def start_next(c):
        @pl.when(c + 1 < CAP)
        def _():
            start_exchange(c + 1)

    def prepare(c):
        @pl.when(c + 2 < CAP)
        def _():
            dispatch(c + 2)

    def start_gather(c):
        take(in_tiles.at[c], e_recv.at[c])
        start_next(c)
        for g in range(2):
            tiles = in_tiles[c, g * SUB : (g + 1) * SUB]
            tx = tiles[:, :TILES].reshape(SUB * TILES, LANE)
            tg = tiles[:, TILES:].reshape(SUB * TILES, LANE)
            both = dot_nn(swap, jnp.concatenate([tx, tg], axis=1)).astype(jnp.bfloat16)
            for j in range(TILES):
                part = both[j * SUB : (j + 1) * SUB]
                rows[c, dp, g * SUB : (g + 1) * SUB, j * LANE : (j + 1) * LANE] = part[:, :LANE]
                rows[c, dp, g * SUB : (g + 1) * SUB, (TILES + j) * LANE : (TILES + j + 1) * LANE] = part[:, LANE:]
        mine = rows.at[c, dp]
        send(mine, mine, a_send.at[c], y_recv.at[c, 0], up)
        send(mine, mine, a_send.at[c], y_recv.at[c, 1], down)
        send(mine, mine, a_send.at[c], c_recv.at[c, 0], twin)

    def forward(c):
        low, high = pl.ds(0, SUB), pl.ds(SUB, SUB)
        take(rows.at[c, d_down], y_recv.at[c, 0])
        block = rows.at[c, d_down, low]
        send(block, block, f_send.at[c], y_recv.at[c, 2], up)
        take(rows.at[c, d_up], y_recv.at[c, 1])
        block = rows.at[c, d_up, high]
        send(block, block, f_send.at[c], y_recv.at[c, 3], down)
        send(rows.at[c, d_down], rows.at[c, d_down], f_send.at[c], c_recv.at[c, 1], twin)
        send(rows.at[c, d_up], rows.at[c, d_up], f_send.at[c], c_recv.at[c, 2], twin)

    def forward_far(c):
        for i in range(2):
            block = rows.at[c, d_far, pl.ds(i * SUB, SUB)]
            take(block, y_recv.at[c, 2 + i])
            send(block, block, h_send.at[c], c_recv.at[c, 3], twin)

    def compute(c):
        t_own, t_down = y * 2 + 1 - k, y_down * 2 + 1 - k
        t_up, t_far = y_up * 2 + 1 - k, y_far * 2 + 1 - k
        for i, d in enumerate((t_own, t_down, t_up, t_far)):
            take(rows.at[c, d], c_recv.at[c, i])

        def hidden(f, _):
            at = pl.ds(pl.multiple_of(f * 256, 256), 256)
            x_rows = rows[c, :, :, :feat].reshape(2 * NY * 32, feat)
            g_rows = rows[c, :, :, feat:].reshape(2 * NY * 32, feat)
            value, slope = gelu_parts(dot_nt(x_rows, w_in[at, :]))
            pre_grad = (dot_nt(g_rows, w_out[at, :]) * slope).astype(jnp.bfloat16)
            act_t[c, at] = value.astype(jnp.bfloat16).T
            pg_t[c, at] = pre_grad.T
            pre_grad = pre_grad.reshape(NY, 2, 32, 256)
            for core in range(2):
                pg[(core + k) % 2, :, :, at] = pre_grad[:, core]
            return 0

        lax.fori_loop(0, hid // 256, hidden, 0)

        def rows_grad(f, _):
            at = pl.ds(pl.multiple_of(f * 512, 512), 512)
            part = dot_nn(pg[...].reshape(2 * NY * 32, hid), w_in[:, at]).reshape(2, NY, 32, 512)
            own[c % 4, :, :, at] = part[0]
            tsend[c, :, :, at] = part[1].astype(jnp.bfloat16)
            return 0

        lax.fori_loop(0, feat // 512, rows_grad, 0)
        send(tsend.at[c], trecv.at[c], t_send.at[c], t_recv.at[c], twin)

    def reduce_far(c):
        take(trecv.at[c], t_recv.at[c])
        o = c % 4
        for i in range(2):
            at = pl.ds(i * SUB, SUB)
            r1s[c, i] = (own[o, y_far, at] + trecv[c, y_far, at].astype(jnp.float32)).astype(jnp.bfloat16)
        send(r1s.at[c, 0], r1r.at[c, 0], r1_send.at[c], r1_recv.at[c, 0], up)
        send(r1s.at[c, 1], r1r.at[c, 1], r1_send.at[c], r1_recv.at[c, 1], down)

    def reduce_near(c):
        o = c % 4
        for i, (to, y_to, first) in enumerate(((up, y_up, 0), (down, y_down, SUB))):
            take(r1r.at[c, i], r1_recv.at[c, i])
            with_far, alone = pl.ds(first, SUB), pl.ds(SUB - first, SUB)
            total = own[o, y_to, with_far] + trecv[c, y_to, with_far].astype(jnp.float32)
            r2s[c, i, with_far] = (total + r1r[c, i].astype(jnp.float32)).astype(jnp.bfloat16)
            total = own[o, y_to, alone] + trecv[c, y_to, alone].astype(jnp.float32)
            r2s[c, i, alone] = total.astype(jnp.bfloat16)
            send(r2s.at[c, i], r2r.at[c, i], r2_send.at[c], r2_recv.at[c, i], to)
        own_sum = own[o, y] + trecv[c, y].astype(jnp.float32)
        own[o, y] = own_sum

    def reduce_last(c):
        o = c % 4
        for i in range(2):
            take(r2r.at[c, i], r2_recv.at[c, i])
        for g in range(2):
            at = pl.ds(g * SUB, SUB)
            total = own[o, y, at] + r2r[c, 0, at].astype(jnp.float32) + r2r[c, 1, at].astype(jnp.float32)
            total = total.astype(jnp.bfloat16)
            out = dot_nn(swap, to_tiles(total, TILES)).astype(jnp.bfloat16)
            fin[c, g * SUB : (g + 1) * SUB] = out.reshape(SUB, TILES, LANE)
        pltpu.make_async_copy(fin.at[c, lang], back.at[c, lang], b_recv.at[c]).start()

        def one(i, _):
            to = (lang + i) % n_hold
            send(fin.at[c, to], back.at[c, lang], b_send.at[c], b_recv.at[c], (dp, to))
            return 0

        lax.fori_loop(1, n_hold, one, 0)

    def finish(c):
        take(back.at[c], b_recv.at[c])
        tall = jnp.concatenate([back[c, g * SUB : (g + 1) * SUB].reshape(SUB * TILES, LANE) for g in range(2)], axis=1)
        flat = dot_nn(swap, tall).astype(jnp.bfloat16)
        for g in range(2):
            for j in range(TILES):
                at = slice(g * LANE, (g + 1) * LANE)
                slots[g * SUB : (g + 1) * SUB, j * LANE : (j + 1) * LANE] = flat[j * SUB : (j + 1) * SUB, at]

        def add(f, _):
            at = pl.ds(pl.multiple_of(f * 512, 512), 512)
            part = lax.dot_general(
                place[c], slots[:, at], (((0,), (0,)), ((), ())), preferred_element_type=jnp.float32
            )
            grad_ref[:, at] = (total_ref[:, at] + part).astype(jnp.bfloat16)
            total_ref[:, at] = total_ref[:, at] + part
            return 0

        lax.fori_loop(0, feat // 512, add, 0)

    def weight_grads(f):
        at = pl.ds(pl.multiple_of(f * 256, 256), 256)
        at_g = pl.ds(pl.multiple_of(feat + f * 256, 256), 256)
        total_in = total_out = None
        for c in range(CAP):
            part_in = dot_nn(pg_t[c], rows[c, :, :, at].reshape(2 * NY * 32, 256))
            part_out = dot_nn(act_t[c], rows[c, :, :, at_g].reshape(2 * NY * 32, 256))
            total_in = part_in if c == 0 else total_in + part_in
            total_out = part_out if c == 0 else total_out + part_out
        gw_in_ref[:, at] = total_in.astype(jnp.bfloat16)
        gw_out_ref[:, at] = total_out.astype(jnp.bfloat16)

    for copy in row_copies:
        copy.wait()
    dispatch(0)
    pl.semaphore_wait(barrier, n_hold - 1 + 3)
    start_exchange(0)
    dispatch(1)
    total_ref[...] = jnp.zeros_like(total_ref)

    stages = [
        (0, start_gather),
        (1, forward),
        (0, prepare),
        (2, compute),
        (1, forward_far),
        (3, reduce_far),
        (4, reduce_near),
        (5, reduce_last),
        (6, finish),
    ]

    def tick(t, _):
        @pl.when(t == 2)
        def _():
            for copy in w_copies:
                copy.wait()

        for offset, stage in stages:
            pl.when((t >= offset) & (t < offset + CAP))(functools.partial(stage, t - offset))

        @pl.when((t >= 7) & (t < 11))
        def _():
            lax.fori_loop(0, 2, lambda i, _: (weight_grads((t - 7) * 2 + i), 0)[1], 0)

        return 0

    lax.fori_loop(0, 6 + CAP, tick, 0)

    def drain(c, _):
        take(in_tiles.at[c, pl.ds(0, n_hold - 1)], e_send.at[c])
        take(rows.at[c, pl.ds(0, 3)], a_send.at[c])
        take(rows.at[c, pl.ds(0, 3)], f_send.at[c])
        take(rows.at[c, 0], h_send.at[c])
        take(tsend.at[c], t_send.at[c])
        take(r1s.at[c], r1_send.at[c])
        take(r2s.at[c], r2_send.at[c])
        take(fin.at[c, pl.ds(0, n_hold - 1)], b_send.at[c])
        return 0

    lax.fori_loop(0, CAP, drain, 0)


def write_out(grad_v, gw_in_v, gw_out_v, grad_h, gw_in_h, gw_out_h, sem):
    copies = [
        pltpu.make_async_copy(src, dst, sem.at[i])
        for i, (src, dst) in enumerate(((grad_v, grad_h), (gw_in_v, gw_in_h), (gw_out_v, gw_out_h)))
    ]
    for copy in copies:
        copy.start()
    for copy in copies:
        copy.wait()


def exchange_and_compute(route, inputs, grad_out, w_first, w_second):
    hid, feat = w_first.shape
    bf16, f32 = jnp.bfloat16, jnp.float32
    n_hold = NX * NZ
    vmem, anywhere = pl.BlockSpec(memory_space=pltpu.VMEM), pl.BlockSpec(memory_space=pl.ANY)
    hbm = pl.BlockSpec(memory_space=pltpu.HBM)
    dma = pltpu.SemaphoreType.DMA
    shapes = (
        jax.ShapeDtypeStruct((inputs.shape[0], feat), bf16),
        jax.ShapeDtypeStruct((hid, feat), bf16),
        jax.ShapeDtypeStruct((hid, feat), bf16),
    )
    made = pl.pallas_call(
        kernel,
        out_shape=shapes,
        in_specs=[vmem, hbm, hbm, hbm, hbm],
        out_specs=(vmem, vmem, vmem),
        scratch_shapes=[
            pltpu.VMEM(inputs.shape, bf16),
            pltpu.VMEM(inputs.shape, bf16),
            pltpu.VMEM((hid, feat), bf16),
            pltpu.VMEM((hid, feat), bf16),
            pltpu.VMEM((CAP, n_hold, 128), bf16),
            pltpu.VMEM((inputs.shape[0], feat), f32),
            pltpu.VMEM((CAP, n_hold, 2 * TILES, LANE), bf16),
            pltpu.VMEM((CAP, n_hold, 2 * TILES, LANE), bf16),
            pltpu.VMEM((CAP, 2 * NY, 32, 2 * feat), bf16),
            pltpu.VMEM((CAP, hid, 256), bf16),
            pltpu.VMEM((CAP, hid, 256), bf16),
            pltpu.VMEM((2, NY, 32, hid), bf16),
            pltpu.VMEM((n_hold, feat), bf16),
            pltpu.VMEM((CAP, NY, 32, feat), bf16),
            pltpu.VMEM((CAP, NY, 32, feat), bf16),
            pltpu.VMEM((4, NY, 32, feat), f32),
            pltpu.VMEM((CAP, 2, SUB, feat), bf16),
            pltpu.VMEM((CAP, 2, SUB, feat), bf16),
            pltpu.VMEM((CAP, 2, 32, feat), bf16),
            pltpu.VMEM((CAP, 2, 32, feat), bf16),
            pltpu.VMEM((CAP, n_hold, TILES, LANE), bf16),
            pltpu.VMEM((CAP, n_hold, TILES, LANE), bf16),
            dma((4,)),
            dma((CAP,)), dma((CAP,)),
            dma((CAP,)), dma((CAP,)), dma((CAP,)),
            dma((CAP, 4)), dma((CAP, 4)),
            dma((CAP,)), dma((CAP,)),
            dma((CAP,)), dma((CAP, 2)),
            dma((CAP,)), dma((CAP, 2)),
            dma((CAP,)), dma((CAP,)),
        ],
        compiler_params=pltpu.CompilerParams(
            collective_id=0, has_side_effects=True, vmem_limit_bytes=48 * 1024 * 1024
        ),
    )(route, inputs, grad_out, w_first, w_second)
    return pl.pallas_call(
        write_out,
        out_shape=shapes,
        in_specs=[vmem] * 3,
        out_specs=(anywhere,) * 3,
        scratch_shapes=[dma((3,))],
        compiler_params=pltpu.CompilerParams(vmem_limit_bytes=1024 * 1024),
    )(*made)


def body(inputs, grad_out, lang_ids, lang_block, block_owner, w_in, w_out):
    lang_row = jnp.pad(lang_block, (0, 256 - lang_block.shape[0]), constant_values=-1)
    owner_row = jnp.pad(block_owner, (0, 128 - block_owner.shape[0]), constant_values=-1)
    route = jnp.concatenate([lang_row, owner_row, lang_ids])[None]
    grad_in, g_in, g_out = exchange_and_compute(route, inputs, grad_out, w_in[0], w_out[0])
    return (grad_in, g_in[None], g_out[None])


def solution(mesh):
    in_specs = (
        P(("dp", "lang"), None),
        P(("dp", "lang"), None),
        P(("dp", "lang")),
        P(),
        P(),
        P("lang", "dp", None),
        P("lang", "dp", None),
    )
    out_specs = (P(("dp", "lang"), None), P("lang", "dp", None), P("lang", "dp", None))
    return jax.shard_map(body, mesh=mesh, in_specs=in_specs, out_specs=out_specs, check_vma=False)
```

```python
import functools
import math

import jax
import jax.numpy as jnp
from jax import lax
from jax.experimental import pallas as pl
from jax.experimental.pallas import tpu as pltpu
from jax.sharding import PartitionSpec as P

gelu_scale = math.sqrt(2.0 / math.pi)
CAP = 5
NX, NZ, NY = 4, 8, 4
LANE = 128
SUB = 16
TILES = 16
MESH = pl.DeviceIdType.MESH


def gelu_parts(pre_act):
    tanh_arg = gelu_scale * (pre_act + 0.044715 * pre_act * pre_act * pre_act)
    tangent = jnp.tanh(tanh_arg)
    gelu_value = 0.5 * pre_act * (1.0 + tangent)
    gelu_slope = 0.5 * (1.0 + tangent) + 0.5 * pre_act * (1.0 - tangent * tangent) * gelu_scale * (
        1.0 + 3.0 * 0.044715 * pre_act * pre_act
    )
    return (gelu_value, gelu_slope)


NEAR = (0, 4)
FAR = (2, 3)
LAST_SLOT = 1


def offset_of(i, far):
    return (i >> 2) & 3, (i & 3) - 1 + 4 * far


def placement(route, x, z, kind):
    n_hold = NX * NZ

    def picks(shape, values):
        at = lax.broadcasted_iota(jnp.int32, shape, 0)
        return jnp.where(at == values, 1.0, 0.0).astype(kind)

    lang_of_row = picks((256, 128), route[:, 384:512])
    block_of_lang = dot_nn(picks((128, 256), route[:, 0:256]), lang_of_row).astype(kind)
    holder = dot_nn(picks((n_hold, 128), route[:, 256:384]), block_of_lang)
    row = lax.broadcasted_iota(jnp.int32, (128, 128), 0)
    later = lax.broadcasted_iota(jnp.int32, (128, 128), 1)
    earlier = dot_nn(holder.astype(kind), jnp.where(row < later, 1.0, 0.0).astype(kind))
    index = lax.broadcasted_iota(jnp.int32, (n_hold, 128), 0)
    holder_of_row = jnp.sum(holder * index.astype(jnp.float32), axis=0, keepdims=True)
    count_of_row = jnp.sum(holder * earlier, axis=0, keepdims=True)
    placed = []
    for c in range(CAP):
        if c == LAST_SLOT:
            peer, far, slot = index & 15, index >> 4, jnp.full_like(index, CAP - 1)
        else:
            peer, far, slot = index >> 1, int(c not in NEAR), (index & 1) + (2 if c in (FAR[1], NEAR[1]) else 0)
        dx, dz = offset_of(peer, far)
        target = ((x + dx) & (NX - 1)) * NZ + ((z + dz + NZ) & (NZ - 1))
        hit = (holder_of_row == target.astype(jnp.float32)) & (count_of_row == slot.astype(jnp.float32))
        placed.append(jnp.where(hit, 1.0, 0.0).astype(kind))
    return placed


def dot_nt(a, b):
    return lax.dot_general(a, b, (((1,), (1,)), ((), ())), preferred_element_type=jnp.float32)


def dot_nn(a, b):
    return lax.dot_general(a, b, (((1,), (0,)), ((), ())), preferred_element_type=jnp.float32)


def kernel(
    route_ref, both_ref, w_in_hbm, w_out_hbm,
    grad_ref, gw_in_ref, gw_out_ref,
    w_in, w_out, place, total_ref, out_tiles, in_tiles, rows, act_t, pg_t, pg, slots, tsend, trecv, own, r1s, r1r, r2s, r2r, fin, back,
    w_sem, e_send, e_recv, a_send, f_send, h_send, y_recv, c_recv,
    t_send, t_recv, r1_send, r1_recv, r2_send, r2_recv, b_send, b_recv,
):
    dp, lang = lax.axis_index("dp"), lax.axis_index("lang")
    y, k = dp // 2, dp % 2
    n_hold = NX * NZ
    x, z = lang // NZ, lang % NZ
    y_up, y_down, y_far = (y + 1) % NY, (y + NY - 1) % NY, (y + 2) % NY
    up, down, twin = (y_up * 2 + k, lang), (y_down * 2 + k, lang), (y * 2 + 1 - k, lang)
    d_up, d_down, d_far = y_up * 2 + k, y_down * 2 + k, y_far * 2 + k
    def send(src, dst, s_sem, r_sem, to):
        pltpu.make_async_remote_copy(
            src_ref=src, dst_ref=dst, send_sem=s_sem, recv_sem=r_sem, device_id=to, device_id_type=MESH
        ).start()

    def take(ref, sem):
        pltpu.make_async_copy(ref, ref, sem).wait()

    w_copies = [
        pltpu.make_async_copy(w_in_hbm, w_in, w_sem.at[0]),
        pltpu.make_async_copy(w_out_hbm, w_out, w_sem.at[1]),
    ]
    for copy in w_copies:
        copy.start()

    barrier = pltpu.get_barrier_semaphore()
    for peer in (up, down, twin):
        pl.semaphore_signal(barrier, inc=1, device_id=peer, device_id_type=MESH)

    def greet(i, _):
        pl.semaphore_signal(barrier, inc=1, device_id=(dp, (lang + i) % n_hold), device_id_type=MESH)
        return 0

    lax.fori_loop(1, n_hold, greet, 0)
    big_row = lax.broadcasted_iota(jnp.int32, (SUB * TILES, SUB * TILES), 0)
    big_col = lax.broadcasted_iota(jnp.int32, (SUB * TILES, SUB * TILES), 1)
    swap = jnp.where(big_col == (big_row % SUB) * TILES + big_row // SUB, 1.0, 0.0).astype(jnp.bfloat16)

    feat = w_in.shape[1]
    hid = w_in.shape[0]
    for slot, picked in enumerate(placement(route_ref[...], x, z, jnp.bfloat16)):
        place[slot] = picked

    def to_tiles(matrix, width):
        return jnp.concatenate([matrix[:, j * LANE : (j + 1) * LANE] for j in range(width)], axis=0)

    def dispatch(c):
        picked = dot_nn(place[c], both_ref[...]).astype(jnp.bfloat16)
        x_rows, g_rows = picked[:, :feat], picked[:, feat:]
        for g in range(2):
            at = slice(g * SUB, (g + 1) * SUB)
            both = jnp.concatenate([to_tiles(x_rows[at], TILES), to_tiles(g_rows[at], TILES)], axis=1)
            both = dot_nn(swap, both).astype(jnp.bfloat16)
            out_tiles[c, at, :TILES] = both[:, :LANE].reshape(SUB, TILES, LANE)
            out_tiles[c, at, TILES:] = both[:, LANE:].reshape(SUB, TILES, LANE)

    x_at = [((x + d) % NX) * NZ for d in range(NX)]
    z_at = [(z + d) % NZ for d in range(NZ)]

    def exchange(c, src, dst, s_sem, r_sem, sign):
        def one(i, at, far):
            dx, dz = offset_of(i, far)
            if dx == 0 and dz == 0:
                pltpu.make_async_copy(src.at[c, at], dst.at[c, at], r_sem.at[c]).start()
            else:
                to = x_at[sign * dx % NX] + z_at[sign * dz % NZ]
                send(src.at[c, at], dst.at[c, at], s_sem.at[c], r_sem.at[c], (dp, to))

        far_first = (2, 1, 3, 0)
        order = [4 * a + b for b in far_first for a in (2, 1, 3, 0)]

        @pl.when((c == NEAR[0]) | (c == NEAR[1]))
        def _():
            for i in order:
                one(i, pl.ds(2 * i, 2), 0)

        @pl.when((c == FAR[0]) | (c == FAR[1]))
        def _():
            for i in order:
                one(i, pl.ds(2 * i, 2), 1)

        @pl.when(c == LAST_SLOT)
        def _():
            for far in (1, 0):
                for i in order:
                    one(i, pl.ds(far * 16 + i, 1), far)

    def sent(c, ref, sem):
        pl.when((c == NEAR[0]) | (c == NEAR[1]))(lambda: take(ref.at[c, pl.ds(0, n_hold - 2)], sem.at[c]))
        pl.when(c == LAST_SLOT)(lambda: take(ref.at[c, pl.ds(0, n_hold - 1)], sem.at[c]))
        pl.when((c == FAR[0]) | (c == FAR[1]))(lambda: take(ref.at[c], sem.at[c]))

    def start_exchange(c):
        exchange(c, out_tiles, in_tiles, e_send, e_recv, 1)

    def start_next(c):
        @pl.when(c + 1 < CAP)
        def _():
            start_exchange(c + 1)

    def prepare(c):
        @pl.when(c + 3 < CAP)
        def _():
            dispatch(c + 3)

    def start_gather(c):
        take(in_tiles.at[c], e_recv.at[c])
        start_next(c)
        for g in range(2):
            tiles = in_tiles[c, g * SUB : (g + 1) * SUB]
            tx = tiles[:, :TILES].reshape(SUB * TILES, LANE)
            tg = tiles[:, TILES:].reshape(SUB * TILES, LANE)
            both = dot_nn(swap, jnp.concatenate([tx, tg], axis=1)).astype(jnp.bfloat16)
            for j in range(TILES):
                part = both[j * SUB : (j + 1) * SUB]
                rows[c, dp, g * SUB : (g + 1) * SUB, j * LANE : (j + 1) * LANE] = part[:, :LANE]
                rows[c, dp, g * SUB : (g + 1) * SUB, (TILES + j) * LANE : (TILES + j + 1) * LANE] = part[:, LANE:]
        mine = rows.at[c, dp]
        send(mine, mine, a_send.at[c], y_recv.at[c, 0], up)
        send(mine, mine, a_send.at[c], y_recv.at[c, 1], down)
        send(mine, mine, a_send.at[c], c_recv.at[c, 0], twin)

    def forward(c):
        low, high = pl.ds(0, SUB), pl.ds(SUB, SUB)
        take(rows.at[c, d_down], y_recv.at[c, 0])
        block = rows.at[c, d_down, low]
        send(block, block, f_send.at[c], y_recv.at[c, 2], up)
        take(rows.at[c, d_up], y_recv.at[c, 1])
        block = rows.at[c, d_up, high]
        send(block, block, f_send.at[c], y_recv.at[c, 3], down)
        send(rows.at[c, d_down], rows.at[c, d_down], f_send.at[c], c_recv.at[c, 1], twin)
        send(rows.at[c, d_up], rows.at[c, d_up], f_send.at[c], c_recv.at[c, 2], twin)

    def forward_far(c):
        for i in range(2):
            block = rows.at[c, d_far, pl.ds(i * SUB, SUB)]
            take(block, y_recv.at[c, 2 + i])
            send(block, block, h_send.at[c], c_recv.at[c, 3], twin)

    def hidden(c, f):
        at = pl.ds(f * 256, 256)
        x_rows = rows[c, :, :, :feat].reshape(2 * NY * 32, feat)
        g_rows = rows[c, :, :, feat:].reshape(2 * NY * 32, feat)
        value, slope = gelu_parts(dot_nt(w_in[at, :], x_rows))
        pre_grad = (dot_nt(w_out[at, :], g_rows) * slope).astype(jnp.bfloat16)
        act_t[c, at] = value.astype(jnp.bfloat16)
        pg_t[c, at] = pre_grad
        pre_grad = pre_grad.T
        pre_grad = pre_grad.reshape(NY, 2, 32, 256)
        for core in range(2):
            pg[(core + k) % 2, :, :, at] = pre_grad[:, core]

    def hidden_low(c):
        t_own, t_down = y * 2 + 1 - k, y_down * 2 + 1 - k
        t_up, t_far = y_up * 2 + 1 - k, y_far * 2 + 1 - k
        for i, d in enumerate((t_own, t_down, t_up, t_far)):
            take(rows.at[c, d], c_recv.at[c, i])
        hidden(c, 0)

    def hidden_high(c):
        hidden(c, 1)

    def rows_grad(c):
        def part_of(f, _):
            at = pl.ds(pl.multiple_of(f * 512, 512), 512)
            part = dot_nn(pg[...].reshape(2 * NY * 32, hid), w_in[:, at]).reshape(2, NY, 32, 512)
            own[c % 4, :, :, at] = part[0]
            tsend[c, :, :, at] = part[1].astype(jnp.bfloat16)
            return 0

        lax.fori_loop(0, feat // 512, part_of, 0)
        send(tsend.at[c], trecv.at[c], t_send.at[c], t_recv.at[c], twin)

    def reduce_far(c):
        take(trecv.at[c], t_recv.at[c])
        o = c % 4
        for i in range(2):
            at = pl.ds(i * SUB, SUB)
            r1s[c, i] = (own[o, y_far, at] + trecv[c, y_far, at].astype(jnp.float32)).astype(jnp.bfloat16)
        send(r1s.at[c, 0], r1r.at[c, 0], r1_send.at[c], r1_recv.at[c, 0], up)
        send(r1s.at[c, 1], r1r.at[c, 1], r1_send.at[c], r1_recv.at[c, 1], down)

    def reduce_near(c):
        o = c % 4
        for i, (to, y_to, first) in enumerate(((up, y_up, 0), (down, y_down, SUB))):
            take(r1r.at[c, i], r1_recv.at[c, i])
            with_far, alone = pl.ds(first, SUB), pl.ds(SUB - first, SUB)
            total = own[o, y_to, with_far] + trecv[c, y_to, with_far].astype(jnp.float32)
            r2s[c, i, with_far] = (total + r1r[c, i].astype(jnp.float32)).astype(jnp.bfloat16)
            total = own[o, y_to, alone] + trecv[c, y_to, alone].astype(jnp.float32)
            r2s[c, i, alone] = total.astype(jnp.bfloat16)
            send(r2s.at[c, i], r2r.at[c, i], r2_send.at[c], r2_recv.at[c, i], to)
        own_sum = own[o, y] + trecv[c, y].astype(jnp.float32)
        own[o, y] = own_sum

    def reduce_last(c):
        o = c % 4
        for i in range(2):
            take(r2r.at[c, i], r2_recv.at[c, i])
        for g in range(2):
            at = pl.ds(g * SUB, SUB)
            total = own[o, y, at] + r2r[c, 0, at].astype(jnp.float32) + r2r[c, 1, at].astype(jnp.float32)
            total = total.astype(jnp.bfloat16)
            out = dot_nn(swap, to_tiles(total, TILES)).astype(jnp.bfloat16)
            fin[c, g * SUB : (g + 1) * SUB] = out.reshape(SUB, TILES, LANE)
        exchange(c, fin, back, b_send, b_recv, -1)

    def finish(c):
        take(back.at[c], b_recv.at[c])
        tall = jnp.concatenate([back[c, g * SUB : (g + 1) * SUB].reshape(SUB * TILES, LANE) for g in range(2)], axis=1)
        flat = dot_nn(swap, tall).astype(jnp.bfloat16)
        for g in range(2):
            for j in range(TILES):
                at = slice(g * LANE, (g + 1) * LANE)
                slots[g * SUB : (g + 1) * SUB, j * LANE : (j + 1) * LANE] = flat[j * SUB : (j + 1) * SUB, at]

        def add(f, _):
            at = pl.ds(pl.multiple_of(f * 512, 512), 512)
            part = lax.dot_general(
                place[c], slots[:, at], (((0,), (0,)), ((), ())), preferred_element_type=jnp.float32
            )
            grad_ref[:, at] = (total_ref[:, at] + part).astype(jnp.bfloat16)
            total_ref[:, at] = total_ref[:, at] + part
            return 0

        lax.fori_loop(0, feat // 512, add, 0)

    def weight_grads(f):
        at = pl.ds(pl.multiple_of(f * 256, 256), 256)
        at_g = pl.ds(pl.multiple_of(feat + f * 256, 256), 256)
        total_in = total_out = None
        for c in range(CAP):
            part_in = dot_nn(pg_t[c], rows[c, :, :, at].reshape(2 * NY * 32, 256))
            part_out = dot_nn(act_t[c], rows[c, :, :, at_g].reshape(2 * NY * 32, 256))
            total_in = part_in if c == 0 else total_in + part_in
            total_out = part_out if c == 0 else total_out + part_out
        gw_in_ref[:, at] = total_in.astype(jnp.bfloat16)
        gw_out_ref[:, at] = total_out.astype(jnp.bfloat16)

    dispatch(0)
    pl.semaphore_wait(barrier, n_hold - 1 + 3)
    start_exchange(0)
    dispatch(1)
    dispatch(2)
    total_ref[...] = jnp.zeros_like(total_ref)

    def outputs(c):
        weight_grads(2 * c)
        weight_grads(2 * c + 1)

    stages = [
        (1, CAP, forward),
        (0, CAP, start_gather),
        (2, CAP, hidden_low),
        (1, CAP, forward_far),
        (2, CAP, hidden_high),
        (3, CAP, reduce_far),
        (2, CAP, rows_grad),
        (4, CAP, reduce_near),
        (0, CAP, prepare),
        (5, CAP, reduce_last),
        (7, 4, outputs),
        (6, CAP, finish),
    ]

    def tick(t, _):
        @pl.when(t == 2)
        def _():
            for copy in w_copies:
                copy.wait()

        for first, count, stage in stages:
            pl.when((t >= first) & (t < first + count))(functools.partial(stage, t - first))

        return 0

    lax.fori_loop(0, 11, tick, 0)

    def drain(c, _):
        sent(c, in_tiles, e_send)
        take(rows.at[c, pl.ds(0, 3)], a_send.at[c])
        take(rows.at[c, pl.ds(0, 3)], f_send.at[c])
        take(rows.at[c, 0], h_send.at[c])
        take(tsend.at[c], t_send.at[c])
        take(r1s.at[c], r1_send.at[c])
        take(r2s.at[c], r2_send.at[c])
        sent(c, fin, b_send)
        return 0

    lax.fori_loop(0, CAP, drain, 0)


def write_out(grad_v, gw_in_v, gw_out_v, grad_h, gw_in_h, gw_out_h, sem):
    copies = [
        pltpu.make_async_copy(src, dst, sem.at[i])
        for i, (src, dst) in enumerate(((grad_v, grad_h), (gw_in_v, gw_in_h), (gw_out_v, gw_out_h)))
    ]
    for copy in copies:
        copy.start()
    for copy in copies:
        copy.wait()


def exchange_and_compute(route, both, w_first, w_second):
    hid, feat = w_first.shape
    bf16, f32 = jnp.bfloat16, jnp.float32
    n_hold = NX * NZ
    vmem, anywhere = pl.BlockSpec(memory_space=pltpu.VMEM), pl.BlockSpec(memory_space=pl.ANY)
    hbm = pl.BlockSpec(memory_space=pltpu.HBM)
    dma = pltpu.SemaphoreType.DMA
    shapes = (
        jax.ShapeDtypeStruct((both.shape[0], feat), bf16),
        jax.ShapeDtypeStruct((hid, feat), bf16),
        jax.ShapeDtypeStruct((hid, feat), bf16),
    )
    made = pl.pallas_call(
        kernel,
        out_shape=shapes,
        in_specs=[vmem, vmem, hbm, hbm],
        out_specs=(vmem, vmem, vmem),
        scratch_shapes=[
            pltpu.VMEM((hid, feat), bf16),
            pltpu.VMEM((hid, feat), bf16),
            pltpu.VMEM((CAP, n_hold, 128), bf16),
            pltpu.VMEM((both.shape[0], feat), f32),
            pltpu.VMEM((CAP, n_hold, 2 * TILES, LANE), bf16),
            pltpu.VMEM((CAP, n_hold, 2 * TILES, LANE), bf16),
            pltpu.VMEM((CAP, 2 * NY, 32, 2 * feat), bf16),
            pltpu.VMEM((CAP, hid, 256), bf16),
            pltpu.VMEM((CAP, hid, 256), bf16),
            pltpu.VMEM((2, NY, 32, hid), bf16),
            pltpu.VMEM((n_hold, feat), bf16),
            pltpu.VMEM((CAP, NY, 32, feat), bf16),
            pltpu.VMEM((CAP, NY, 32, feat), bf16),
            pltpu.VMEM((4, NY, 32, feat), f32),
            pltpu.VMEM((CAP, 2, SUB, feat), bf16),
            pltpu.VMEM((CAP, 2, SUB, feat), bf16),
            pltpu.VMEM((CAP, 2, 32, feat), bf16),
            pltpu.VMEM((CAP, 2, 32, feat), bf16),
            pltpu.VMEM((CAP, n_hold, TILES, LANE), bf16),
            pltpu.VMEM((CAP, n_hold, TILES, LANE), bf16),
            dma((2,)),
            dma((CAP,)), dma((CAP,)),
            dma((CAP,)), dma((CAP,)), dma((CAP,)),
            dma((CAP, 4)), dma((CAP, 4)),
            dma((CAP,)), dma((CAP,)),
            dma((CAP,)), dma((CAP, 2)),
            dma((CAP,)), dma((CAP, 2)),
            dma((CAP,)), dma((CAP,)),
        ],
        compiler_params=pltpu.CompilerParams(
            collective_id=0, has_side_effects=True, vmem_limit_bytes=48 * 1024 * 1024
        ),
    )(route, both, w_first, w_second)
    return pl.pallas_call(
        write_out,
        out_shape=shapes,
        in_specs=[vmem] * 3,
        out_specs=(anywhere,) * 3,
        scratch_shapes=[dma((3,))],
        compiler_params=pltpu.CompilerParams(vmem_limit_bytes=1024 * 1024),
    )(*made)


def body(inputs, grad_out, lang_ids, lang_block, block_owner, w_in, w_out):
    lang_row = jnp.pad(lang_block, (0, 256 - lang_block.shape[0]), constant_values=-1)
    owner_row = jnp.pad(block_owner, (0, 128 - block_owner.shape[0]), constant_values=-1)
    route = jnp.concatenate([lang_row, owner_row, lang_ids])[None]
    grad_in, g_in, g_out = exchange_and_compute(route, jnp.concatenate([inputs, grad_out], axis=1), w_in[0], w_out[0])
    return (grad_in, g_in[None], g_out[None])


def solution(mesh):
    in_specs = (
        P(("dp", "lang"), None),
        P(("dp", "lang"), None),
        P(("dp", "lang")),
        P(),
        P(),
        P("lang", "dp", None),
        P("lang", "dp", None),
    )
    out_specs = (P(("dp", "lang"), None), P("lang", "dp", None), P("lang", "dp", None))
    return jax.shard_map(body, mesh=mesh, in_specs=in_specs, out_specs=out_specs, check_vma=False)
```

```python
import functools
import math

import jax
import jax.numpy as jnp
from jax import lax
from jax.experimental import pallas as pl
from jax.experimental.pallas import tpu as pltpu
from jax.sharding import PartitionSpec as P

gelu_scale = math.sqrt(2.0 / math.pi)
CAP = 5
NX, NZ, NY = 4, 8, 4
LANE = 128
SUB = 16
TILES = 16
MESH = pl.DeviceIdType.MESH


def gelu_parts(pre_act):
    tanh_arg = gelu_scale * (pre_act + 0.044715 * pre_act * pre_act * pre_act)
    tangent = jnp.tanh(tanh_arg)
    gelu_value = 0.5 * pre_act * (1.0 + tangent)
    gelu_slope = 0.5 * (1.0 + tangent) + 0.5 * pre_act * (1.0 - tangent * tangent) * gelu_scale * (
        1.0 + 3.0 * 0.044715 * pre_act * pre_act
    )
    return (gelu_value, gelu_slope)


NEAR = (0, 4)
FAR = (2, 3)
LAST_SLOT = 1


def offset_of(i, far):
    return (i >> 2) & 3, (i & 3) - 1 + 4 * far


def placement(route, x, z, kind):
    n_hold = NX * NZ

    def picks(shape, values):
        at = lax.broadcasted_iota(jnp.int32, shape, 0)
        return jnp.where(at == values, 1.0, 0.0).astype(kind)

    lang_of_row = picks((256, 128), route[:, 384:512])
    block_of_lang = dot_nn(picks((128, 256), route[:, 0:256]), lang_of_row).astype(kind)
    holder = dot_nn(picks((n_hold, 128), route[:, 256:384]), block_of_lang)
    row = lax.broadcasted_iota(jnp.int32, (128, 128), 0)
    later = lax.broadcasted_iota(jnp.int32, (128, 128), 1)
    earlier = dot_nn(holder.astype(kind), jnp.where(row < later, 1.0, 0.0).astype(kind))
    index = lax.broadcasted_iota(jnp.int32, (n_hold, 128), 0)
    holder_of_row = jnp.sum(holder * index.astype(jnp.float32), axis=0, keepdims=True)
    count_of_row = jnp.sum(holder * earlier, axis=0, keepdims=True)
    placed = []
    for c in range(CAP):
        if c == LAST_SLOT:
            peer, far, slot = index & 15, index >> 4, jnp.full_like(index, CAP - 1)
        else:
            peer, far, slot = index >> 1, int(c not in NEAR), (index & 1) + (2 if c in (FAR[1], NEAR[1]) else 0)
        dx, dz = offset_of(peer, far)
        target = ((x + dx) & (NX - 1)) * NZ + ((z + dz + NZ) & (NZ - 1))
        hit = (holder_of_row == target.astype(jnp.float32)) & (count_of_row == slot.astype(jnp.float32))
        placed.append(jnp.where(hit, 1.0, 0.0).astype(kind))
    return placed


def dot_nt(a, b):
    return lax.dot_general(a, b, (((1,), (1,)), ((), ())), preferred_element_type=jnp.float32)


def dot_nn(a, b):
    return lax.dot_general(a, b, (((1,), (0,)), ((), ())), preferred_element_type=jnp.float32)


def kernel(
    route_ref, both_ref, w_in_hbm, w_out_hbm,
    grad_ref, gw_in_ref, gw_out_ref,
    w_in, w_out, place, out_tiles, in_tiles, rows, act_t, pg_t, pg, slots, tsend, trecv, own, r1s, r1r, r2s, r2r, fin, back,
    w_sem, e_send, e_recv, a_send, f_send, h_send, y_recv, c_recv,
    t_send, t_recv, r1_send, r1_recv, r2_send, r2_recv, b_send, b_recv,
):
    dp, lang = lax.axis_index("dp"), lax.axis_index("lang")
    y, k = dp // 2, dp % 2
    n_hold = NX * NZ
    x, z = lang // NZ, lang % NZ
    y_up, y_down, y_far = (y + 1) % NY, (y + NY - 1) % NY, (y + 2) % NY
    up, down, twin = (y_up * 2 + k, lang), (y_down * 2 + k, lang), (y * 2 + 1 - k, lang)
    d_up, d_down, d_far = y_up * 2 + k, y_down * 2 + k, y_far * 2 + k
    def send(src, dst, s_sem, r_sem, to):
        pltpu.make_async_remote_copy(
            src_ref=src, dst_ref=dst, send_sem=s_sem, recv_sem=r_sem, device_id=to, device_id_type=MESH
        ).start()

    def take(ref, sem):
        pltpu.make_async_copy(ref, ref, sem).wait()

    w_copies = [
        pltpu.make_async_copy(w_in_hbm, w_in, w_sem.at[0]),
        pltpu.make_async_copy(w_out_hbm, w_out, w_sem.at[1]),
    ]
    for copy in w_copies:
        copy.start()

    barrier = pltpu.get_barrier_semaphore()
    for peer in (up, down, twin):
        pl.semaphore_signal(barrier, inc=1, device_id=peer, device_id_type=MESH)

    def greet(i, _):
        pl.semaphore_signal(barrier, inc=1, device_id=(dp, (lang + i) % n_hold), device_id_type=MESH)
        return 0

    lax.fori_loop(1, n_hold, greet, 0)
    big_row = lax.broadcasted_iota(jnp.int32, (SUB * TILES, SUB * TILES), 0)
    big_col = lax.broadcasted_iota(jnp.int32, (SUB * TILES, SUB * TILES), 1)
    swap = jnp.where(big_col == (big_row % SUB) * TILES + big_row // SUB, 1.0, 0.0).astype(jnp.bfloat16)

    feat = w_in.shape[1]
    hid = w_in.shape[0]
    for slot, picked in enumerate(placement(route_ref[...], x, z, jnp.bfloat16)):
        place[slot] = picked

    def to_tiles(matrix, width):
        return jnp.concatenate([matrix[:, j * LANE : (j + 1) * LANE] for j in range(width)], axis=0)

    def dispatch(c):
        picked = dot_nn(place[c], both_ref[...]).astype(jnp.bfloat16)
        x_rows, g_rows = picked[:, :feat], picked[:, feat:]
        for g in range(2):
            at = slice(g * SUB, (g + 1) * SUB)
            both = jnp.concatenate([to_tiles(x_rows[at], TILES), to_tiles(g_rows[at], TILES)], axis=1)
            both = dot_nn(swap, both).astype(jnp.bfloat16)
            out_tiles[c, at, :TILES] = both[:, :LANE].reshape(SUB, TILES, LANE)
            out_tiles[c, at, TILES:] = both[:, LANE:].reshape(SUB, TILES, LANE)

    x_at = [((x + d) % NX) * NZ for d in range(NX)]
    z_at = [(z + d) % NZ for d in range(NZ)]

    def exchange(c, src, dst, s_sem, r_sem, sign):
        def one(i, at, far):
            dx, dz = offset_of(i, far)
            if dx == 0 and dz == 0:
                pltpu.make_async_copy(src.at[c, at], dst.at[c, at], r_sem.at[c]).start()
            else:
                to = x_at[sign * dx % NX] + z_at[sign * dz % NZ]
                send(src.at[c, at], dst.at[c, at], s_sem.at[c], r_sem.at[c], (dp, to))

        far_first = (2, 1, 3, 0)
        order = [4 * a + b for b in far_first for a in (2, 1, 3, 0)]

        @pl.when((c == NEAR[0]) | (c == NEAR[1]))
        def _():
            for i in order:
                one(i, pl.ds(2 * i, 2), 0)

        @pl.when((c == FAR[0]) | (c == FAR[1]))
        def _():
            for i in order:
                one(i, pl.ds(2 * i, 2), 1)

        @pl.when(c == LAST_SLOT)
        def _():
            for far in (1, 0):
                for i in order:
                    one(i, pl.ds(far * 16 + i, 1), far)

    def sent(c, ref, sem):
        pl.when((c == NEAR[0]) | (c == NEAR[1]))(lambda: take(ref.at[c, pl.ds(0, n_hold - 2)], sem.at[c]))
        pl.when(c == LAST_SLOT)(lambda: take(ref.at[c, pl.ds(0, n_hold - 1)], sem.at[c]))
        pl.when((c == FAR[0]) | (c == FAR[1]))(lambda: take(ref.at[c], sem.at[c]))

    def start_exchange(c):
        exchange(c, out_tiles, in_tiles, e_send, e_recv, 1)

    def start_next(c):
        @pl.when(c + 1 < CAP)
        def _():
            start_exchange(c + 1)

    def prepare(c):
        @pl.when(c + 3 < CAP)
        def _():
            dispatch(c + 3)

    def start_gather(c):
        take(in_tiles.at[c], e_recv.at[c])
        start_next(c)
        for g in range(2):
            tiles = in_tiles[c, g * SUB : (g + 1) * SUB]
            tx = tiles[:, :TILES].reshape(SUB * TILES, LANE)
            tg = tiles[:, TILES:].reshape(SUB * TILES, LANE)
            both = dot_nn(swap, jnp.concatenate([tx, tg], axis=1)).astype(jnp.bfloat16)
            for j in range(TILES):
                part = both[j * SUB : (j + 1) * SUB]
                rows[c, dp, g * SUB : (g + 1) * SUB, j * LANE : (j + 1) * LANE] = part[:, :LANE]
                rows[c, dp, g * SUB : (g + 1) * SUB, (TILES + j) * LANE : (TILES + j + 1) * LANE] = part[:, LANE:]
        mine = rows.at[c, dp]
        send(mine, mine, a_send.at[c], y_recv.at[c, 0], up)
        send(mine, mine, a_send.at[c], y_recv.at[c, 1], down)
        send(mine, mine, a_send.at[c], c_recv.at[c, 0], twin)

    def forward(c):
        low, high = pl.ds(0, SUB), pl.ds(SUB, SUB)
        take(rows.at[c, d_down], y_recv.at[c, 0])
        block = rows.at[c, d_down, low]
        send(block, block, f_send.at[c], y_recv.at[c, 2], up)
        take(rows.at[c, d_up], y_recv.at[c, 1])
        block = rows.at[c, d_up, high]
        send(block, block, f_send.at[c], y_recv.at[c, 3], down)
        send(rows.at[c, d_down], rows.at[c, d_down], f_send.at[c], c_recv.at[c, 1], twin)
        send(rows.at[c, d_up], rows.at[c, d_up], f_send.at[c], c_recv.at[c, 2], twin)

    def forward_far(c):
        for i in range(2):
            block = rows.at[c, d_far, pl.ds(i * SUB, SUB)]
            take(block, y_recv.at[c, 2 + i])
            send(block, block, h_send.at[c], c_recv.at[c, 3], twin)

    def hidden(c, f):
        at = pl.ds(f * 256, 256)
        x_rows = rows[c, :, :, :feat].reshape(2 * NY * 32, feat)
        g_rows = rows[c, :, :, feat:].reshape(2 * NY * 32, feat)
        value, slope = gelu_parts(dot_nt(w_in[at, :], x_rows))
        pre_grad = (dot_nt(w_out[at, :], g_rows) * slope).astype(jnp.bfloat16)
        act_t[c, at] = value.astype(jnp.bfloat16)
        pg_t[c, at] = pre_grad
        pre_grad = pre_grad.T
        pre_grad = pre_grad.reshape(NY, 2, 32, 256)
        for core in range(2):
            pg[(core + k) % 2, :, :, at] = pre_grad[:, core]

    def hidden_low(c):
        t_own, t_down = y * 2 + 1 - k, y_down * 2 + 1 - k
        t_up, t_far = y_up * 2 + 1 - k, y_far * 2 + 1 - k
        for i, d in enumerate((t_own, t_down, t_up, t_far)):
            take(rows.at[c, d], c_recv.at[c, i])
        hidden(c, 0)

    def hidden_high(c):
        hidden(c, 1)

    def rows_grad(c):
        def part_of(f, _):
            at = pl.ds(pl.multiple_of(f * 512, 512), 512)
            part = dot_nn(pg[...].reshape(2 * NY * 32, hid), w_in[:, at]).reshape(2, NY, 32, 512)
            own[c % 4, :, :, at] = part[0]
            tsend[c, :, :, at] = part[1].astype(jnp.bfloat16)
            return 0

        lax.fori_loop(0, feat // 512, part_of, 0)
        send(tsend.at[c], trecv.at[c], t_send.at[c], t_recv.at[c], twin)

    def reduce_far(c):
        take(trecv.at[c], t_recv.at[c])
        o = c % 4
        for i in range(2):
            at = pl.ds(i * SUB, SUB)
            r1s[c, i] = (own[o, y_far, at] + trecv[c, y_far, at].astype(jnp.float32)).astype(jnp.bfloat16)
        send(r1s.at[c, 0], r1r.at[c, 0], r1_send.at[c], r1_recv.at[c, 0], up)
        send(r1s.at[c, 1], r1r.at[c, 1], r1_send.at[c], r1_recv.at[c, 1], down)

    def reduce_near(c):
        o = c % 4
        for i, (to, y_to, first) in enumerate(((up, y_up, 0), (down, y_down, SUB))):
            take(r1r.at[c, i], r1_recv.at[c, i])
            with_far, alone = pl.ds(first, SUB), pl.ds(SUB - first, SUB)
            total = own[o, y_to, with_far] + trecv[c, y_to, with_far].astype(jnp.float32)
            r2s[c, i, with_far] = (total + r1r[c, i].astype(jnp.float32)).astype(jnp.bfloat16)
            total = own[o, y_to, alone] + trecv[c, y_to, alone].astype(jnp.float32)
            r2s[c, i, alone] = total.astype(jnp.bfloat16)
            send(r2s.at[c, i], r2r.at[c, i], r2_send.at[c], r2_recv.at[c, i], to)
        own_sum = own[o, y] + trecv[c, y].astype(jnp.float32)
        own[o, y] = own_sum

    def reduce_last(c):
        o = c % 4
        for i in range(2):
            take(r2r.at[c, i], r2_recv.at[c, i])
        for g in range(2):
            at = pl.ds(g * SUB, SUB)
            total = own[o, y, at] + r2r[c, 0, at].astype(jnp.float32) + r2r[c, 1, at].astype(jnp.float32)
            total = total.astype(jnp.bfloat16)
            out = dot_nn(swap, to_tiles(total, TILES)).astype(jnp.bfloat16)
            fin[c, g * SUB : (g + 1) * SUB] = out.reshape(SUB, TILES, LANE)
        exchange(c, fin, back, b_send, b_recv, -1)

    def finish(c):
        take(back.at[c], b_recv.at[c])
        tall = jnp.concatenate([back[c, g * SUB : (g + 1) * SUB].reshape(SUB * TILES, LANE) for g in range(2)], axis=1)
        flat = dot_nn(swap, tall).astype(jnp.bfloat16)
        for g in range(2):
            for j in range(TILES):
                at = slice(g * LANE, (g + 1) * LANE)
                slots[c, g * SUB : (g + 1) * SUB, j * LANE : (j + 1) * LANE] = flat[j * SUB : (j + 1) * SUB, at]

        @pl.when(c == CAP - 1)
        def _():
            def combine(f, _):
                at = pl.ds(pl.multiple_of(f * 512, 512), 512)
                grad = lax.dot_general(
                    place[...].reshape(CAP * n_hold, LANE), slots[:, :, at].reshape(CAP * n_hold, 512),
                    (((0,), (0,)), ((), ())), preferred_element_type=jnp.float32,
                )
                grad_ref[:, at] = grad.astype(jnp.bfloat16)
                return 0

            lax.fori_loop(0, feat // 512, combine, 0)

    def weight_grads(f):
        at = pl.ds(pl.multiple_of(f * 256, 256), 256)
        at_g = pl.ds(pl.multiple_of(feat + f * 256, 256), 256)
        total_in = total_out = None
        for c in range(CAP):
            part_in = dot_nn(pg_t[c], rows[c, :, :, at].reshape(2 * NY * 32, 256))
            part_out = dot_nn(act_t[c], rows[c, :, :, at_g].reshape(2 * NY * 32, 256))
            total_in = part_in if c == 0 else total_in + part_in
            total_out = part_out if c == 0 else total_out + part_out
        gw_in_ref[:, at] = total_in.astype(jnp.bfloat16)
        gw_out_ref[:, at] = total_out.astype(jnp.bfloat16)

    dispatch(0)
    pl.semaphore_wait(barrier, n_hold - 1 + 3)
    start_exchange(0)
    dispatch(1)
    dispatch(2)

    def outputs(c):
        weight_grads(2 * c)
        weight_grads(2 * c + 1)

    stages = [
        (1, CAP, forward),
        (0, CAP, start_gather),
        (2, CAP, hidden_low),
        (1, CAP, forward_far),
        (2, CAP, hidden_high),
        (3, CAP, reduce_far),
        (2, CAP, rows_grad),
        (4, CAP, reduce_near),
        (0, CAP, prepare),
        (5, CAP, reduce_last),
        (7, 4, outputs),
        (6, CAP, finish),
    ]

    def tick(t, _):
        @pl.when(t == 2)
        def _():
            for copy in w_copies:
                copy.wait()

        for first, count, stage in stages:
            pl.when((t >= first) & (t < first + count))(functools.partial(stage, t - first))

        return 0

    lax.fori_loop(0, 11, tick, 0)

    def drain(c, _):
        sent(c, in_tiles, e_send)
        take(rows.at[c, pl.ds(0, 3)], a_send.at[c])
        take(rows.at[c, pl.ds(0, 3)], f_send.at[c])
        take(rows.at[c, 0], h_send.at[c])
        take(tsend.at[c], t_send.at[c])
        take(r1s.at[c], r1_send.at[c])
        take(r2s.at[c], r2_send.at[c])
        sent(c, fin, b_send)
        return 0

    lax.fori_loop(0, CAP, drain, 0)


def write_out(grad_v, gw_in_v, gw_out_v, grad_h, gw_in_h, gw_out_h, sem):
    rows = grad_v.shape[0]
    parts = [(grad_v, grad_h, 0)]
    for first in range(0, gw_in_v.shape[0], rows):
        parts += [(gw_in_v, gw_in_h, first), (gw_out_v, gw_out_h, first)]
    copies = [
        pltpu.make_async_copy(src.at[pl.ds(first, rows)], dst.at[pl.ds(first, rows)], sem.at[i])
        for i, (src, dst, first) in enumerate(parts)
    ]
    for copy in copies:
        copy.start()
    for copy in copies:
        copy.wait()


def exchange_and_compute(route, both, w_first, w_second):
    hid, feat = w_first.shape
    bf16, f32 = jnp.bfloat16, jnp.float32
    n_hold = NX * NZ
    vmem, anywhere = pl.BlockSpec(memory_space=pltpu.VMEM), pl.BlockSpec(memory_space=pl.ANY)
    hbm = pl.BlockSpec(memory_space=pltpu.HBM)
    dma = pltpu.SemaphoreType.DMA
    shapes = (
        jax.ShapeDtypeStruct((both.shape[0], feat), bf16),
        jax.ShapeDtypeStruct((hid, feat), bf16),
        jax.ShapeDtypeStruct((hid, feat), bf16),
    )
    made = pl.pallas_call(
        kernel,
        out_shape=shapes,
        in_specs=[vmem, vmem, hbm, hbm],
        out_specs=(vmem, vmem, vmem),
        scratch_shapes=[
            pltpu.VMEM((hid, feat), bf16),
            pltpu.VMEM((hid, feat), bf16),
            pltpu.VMEM((CAP, n_hold, 128), bf16),
            pltpu.VMEM((CAP, n_hold, 2 * TILES, LANE), bf16),
            pltpu.VMEM((CAP, n_hold, 2 * TILES, LANE), bf16),
            pltpu.VMEM((CAP, 2 * NY, 32, 2 * feat), bf16),
            pltpu.VMEM((CAP, hid, 256), bf16),
            pltpu.VMEM((CAP, hid, 256), bf16),
            pltpu.VMEM((2, NY, 32, hid), bf16),
            pltpu.VMEM((CAP, n_hold, feat), bf16),
            pltpu.VMEM((CAP, NY, 32, feat), bf16),
            pltpu.VMEM((CAP, NY, 32, feat), bf16),
            pltpu.VMEM((4, NY, 32, feat), f32),
            pltpu.VMEM((CAP, 2, SUB, feat), bf16),
            pltpu.VMEM((CAP, 2, SUB, feat), bf16),
            pltpu.VMEM((CAP, 2, 32, feat), bf16),
            pltpu.VMEM((CAP, 2, 32, feat), bf16),
            pltpu.VMEM((CAP, n_hold, TILES, LANE), bf16),
            pltpu.VMEM((CAP, n_hold, TILES, LANE), bf16),
            dma((2,)),
            dma((CAP,)), dma((CAP,)),
            dma((CAP,)), dma((CAP,)), dma((CAP,)),
            dma((CAP, 4)), dma((CAP, 4)),
            dma((CAP,)), dma((CAP,)),
            dma((CAP,)), dma((CAP, 2)),
            dma((CAP,)), dma((CAP, 2)),
            dma((CAP,)), dma((CAP,)),
        ],
        compiler_params=pltpu.CompilerParams(
            collective_id=0, has_side_effects=True, vmem_limit_bytes=48 * 1024 * 1024
        ),
    )(route, both, w_first, w_second)
    return pl.pallas_call(
        write_out,
        out_shape=shapes,
        in_specs=[vmem] * 3,
        out_specs=(anywhere,) * 3,
        scratch_shapes=[dma((1 + 2 * hid // both.shape[0],))],
        compiler_params=pltpu.CompilerParams(vmem_limit_bytes=1024 * 1024),
    )(*made)


def body(inputs, grad_out, lang_ids, lang_block, block_owner, w_in, w_out):
    lang_row = jnp.pad(lang_block, (0, 256 - lang_block.shape[0]), constant_values=-1)
    owner_row = jnp.pad(block_owner, (0, 128 - block_owner.shape[0]), constant_values=-1)
    route = jnp.concatenate([lang_row, owner_row, lang_ids])[None]
    grad_in, g_in, g_out = exchange_and_compute(route, jnp.concatenate([inputs, grad_out], axis=1), w_in[0], w_out[0])
    return (grad_in, g_in[None], g_out[None])


def solution(mesh):
    in_specs = (
        P(("dp", "lang"), None),
        P(("dp", "lang"), None),
        P(("dp", "lang")),
        P(),
        P(),
        P("lang", "dp", None),
        P("lang", "dp", None),
    )
    out_specs = (P(("dp", "lang"), None), P("lang", "dp", None), P("lang", "dp", None))
    return jax.shard_map(body, mesh=mesh, in_specs=in_specs, out_specs=out_specs, check_vma=False)
```

```python
import functools
import math

import jax
import jax.numpy as jnp
from jax import lax
from jax.experimental import pallas as pl
from jax.experimental.pallas import tpu as pltpu
from jax.sharding import PartitionSpec as P

gelu_scale = math.sqrt(2.0 / math.pi)
CAP = 5
NX, NZ, NY = 4, 8, 4
LANE = 128
SUB = 16
TILES = 16
MESH = pl.DeviceIdType.MESH


def gelu_parts(pre_act):
    tanh_arg = gelu_scale * (pre_act + 0.044715 * pre_act * pre_act * pre_act)
    tangent = jnp.tanh(tanh_arg)
    gelu_value = 0.5 * pre_act * (1.0 + tangent)
    gelu_slope = 0.5 * (1.0 + tangent) + 0.5 * pre_act * (1.0 - tangent * tangent) * gelu_scale * (
        1.0 + 3.0 * 0.044715 * pre_act * pre_act
    )
    return (gelu_value, gelu_slope)


NEAR = (0, 4)
FAR = (2, 3)
LAST_SLOT = 1


def offset_of(i, far):
    return (i >> 2) & 3, (i & 3) - 1 + 4 * far


def placement(route, x, z, kind):
    n_hold = NX * NZ

    def picks(shape, values):
        at = lax.broadcasted_iota(jnp.int32, shape, 0)
        return jnp.where(at == values, 1.0, 0.0).astype(kind)

    lang_of_row = picks((256, 128), route[:, 384:512])
    block_of_lang = dot_nn(picks((128, 256), route[:, 0:256]), lang_of_row).astype(kind)
    holder = dot_nn(picks((n_hold, 128), route[:, 256:384]), block_of_lang)
    row = lax.broadcasted_iota(jnp.int32, (128, 128), 0)
    later = lax.broadcasted_iota(jnp.int32, (128, 128), 1)
    earlier = dot_nn(holder.astype(kind), jnp.where(row < later, 1.0, 0.0).astype(kind))
    index = lax.broadcasted_iota(jnp.int32, (n_hold, 128), 0)
    holder_of_row = jnp.sum(holder * index.astype(jnp.float32), axis=0, keepdims=True)
    count_of_row = jnp.sum(holder * earlier, axis=0, keepdims=True)
    placed = []
    for c in range(CAP):
        if c == LAST_SLOT:
            peer, far, slot = index & 15, index >> 4, jnp.full_like(index, CAP - 1)
        else:
            peer, far, slot = index >> 1, int(c not in NEAR), (index & 1) + (2 if c in (FAR[1], NEAR[1]) else 0)
        dx, dz = offset_of(peer, far)
        target = ((x + dx) & (NX - 1)) * NZ + ((z + dz + NZ) & (NZ - 1))
        hit = (holder_of_row == target.astype(jnp.float32)) & (count_of_row == slot.astype(jnp.float32))
        placed.append(jnp.where(hit, 1.0, 0.0).astype(kind))
    return placed


def dot_nt(a, b):
    return lax.dot_general(a, b, (((1,), (1,)), ((), ())), preferred_element_type=jnp.float32)


def dot_nn(a, b):
    return lax.dot_general(a, b, (((1,), (0,)), ((), ())), preferred_element_type=jnp.float32)


def kernel(
    route_ref, both_ref, w_in_hbm, w_out_hbm,
    grad_ref, gw_in_ref, gw_out_ref,
    w_in, w_out, place, out_tiles, in_tiles, rows, act_t, pg_t, pg, slots, tsend, trecv, own, r1s, r1r, r2s, r2r, fin, back,
    w_sem, e_send, e_recv, a_send, f_send, h_send, y_recv, c_recv,
    t_send, t_recv, r1_send, r1_recv, r2_send, r2_recv, b_send, b_recv,
):
    dp, lang = lax.axis_index("dp"), lax.axis_index("lang")
    y, k = dp // 2, dp % 2
    n_hold = NX * NZ
    x, z = lang // NZ, lang % NZ
    y_up, y_down, y_far = (y + 1) % NY, (y + NY - 1) % NY, (y + 2) % NY
    up, down, twin = (y_up * 2 + k, lang), (y_down * 2 + k, lang), (y * 2 + 1 - k, lang)
    d_up, d_down, d_far = y_up * 2 + k, y_down * 2 + k, y_far * 2 + k
    def send(src, dst, s_sem, r_sem, to):
        pltpu.make_async_remote_copy(
            src_ref=src, dst_ref=dst, send_sem=s_sem, recv_sem=r_sem, device_id=to, device_id_type=MESH
        ).start()

    def take(ref, sem):
        pltpu.make_async_copy(ref, ref, sem).wait()

    w_copies = [
        pltpu.make_async_copy(w_in_hbm, w_in, w_sem.at[0]),
        pltpu.make_async_copy(w_out_hbm, w_out, w_sem.at[1]),
    ]
    for copy in w_copies:
        copy.start()

    barrier = pltpu.get_barrier_semaphore()
    for peer in (up, down, twin):
        pl.semaphore_signal(barrier, inc=1, device_id=peer, device_id_type=MESH)

    def greet(i, _):
        pl.semaphore_signal(barrier, inc=1, device_id=(dp, (lang + i) % n_hold), device_id_type=MESH)
        return 0

    lax.fori_loop(1, n_hold, greet, 0)
    big_row = lax.broadcasted_iota(jnp.int32, (SUB * TILES, SUB * TILES), 0)
    big_col = lax.broadcasted_iota(jnp.int32, (SUB * TILES, SUB * TILES), 1)
    swap = jnp.where(big_col == (big_row % SUB) * TILES + big_row // SUB, 1.0, 0.0).astype(jnp.bfloat16)

    feat = w_in.shape[1]
    hid = w_in.shape[0]
    for slot, picked in enumerate(placement(route_ref[...], x, z, jnp.bfloat16)):
        place[slot] = picked

    def to_tiles(matrix, width):
        return jnp.concatenate([matrix[:, j * LANE : (j + 1) * LANE] for j in range(width)], axis=0)

    def dispatch(c):
        picked = dot_nn(place[c], both_ref[...]).astype(jnp.bfloat16)
        x_rows, g_rows = picked[:, :feat], picked[:, feat:]
        for g in range(2):
            at = slice(g * SUB, (g + 1) * SUB)
            both = jnp.concatenate([to_tiles(x_rows[at], TILES), to_tiles(g_rows[at], TILES)], axis=1)
            both = dot_nn(swap, both).astype(jnp.bfloat16)
            out_tiles[c, at, :TILES] = both[:, :LANE].reshape(SUB, TILES, LANE)
            out_tiles[c, at, TILES:] = both[:, LANE:].reshape(SUB, TILES, LANE)

    x_at = [((x + d) % NX) * NZ for d in range(NX)]
    z_at = [(z + d) % NZ for d in range(NZ)]

    def exchange(c, src, dst, s_sem, r_sem, sign):
        def one(i, at, far):
            dx, dz = offset_of(i, far)
            if dx == 0 and dz == 0:
                pltpu.make_async_copy(src.at[c, at], dst.at[c, at], r_sem.at[c]).start()
            else:
                to = x_at[sign * dx % NX] + z_at[sign * dz % NZ]
                send(src.at[c, at], dst.at[c, at], s_sem.at[c], r_sem.at[c], (dp, to))

        far_first = (2, 1, 3, 0)
        order = [4 * a + b for b in far_first for a in (2, 1, 3, 0)]

        @pl.when((c == NEAR[0]) | (c == NEAR[1]))
        def _():
            for i in order:
                one(i, pl.ds(2 * i, 2), 0)

        @pl.when((c == FAR[0]) | (c == FAR[1]))
        def _():
            for i in order:
                one(i, pl.ds(2 * i, 2), 1)

        @pl.when(c == LAST_SLOT)
        def _():
            for far in (1, 0):
                for i in order:
                    one(i, pl.ds(far * 16 + i, 1), far)

    def sent(c, ref, sem):
        pl.when((c == NEAR[0]) | (c == NEAR[1]))(lambda: take(ref.at[c, pl.ds(0, n_hold - 2)], sem.at[c]))
        pl.when(c == LAST_SLOT)(lambda: take(ref.at[c, pl.ds(0, n_hold - 1)], sem.at[c]))
        pl.when((c == FAR[0]) | (c == FAR[1]))(lambda: take(ref.at[c], sem.at[c]))

    def start_exchange(c):
        exchange(c, out_tiles, in_tiles, e_send, e_recv, 1)

    def start_next(c):
        @pl.when(c + 1 < CAP)
        def _():
            start_exchange(c + 1)

    def prepare(c):
        @pl.when(c + 3 < CAP)
        def _():
            dispatch(c + 3)

    def start_gather(c):
        take(in_tiles.at[c], e_recv.at[c])
        start_next(c)
        for g in range(2):
            tiles = in_tiles[c, g * SUB : (g + 1) * SUB]
            tx = tiles[:, :TILES].reshape(SUB * TILES, LANE)
            tg = tiles[:, TILES:].reshape(SUB * TILES, LANE)
            both = dot_nn(swap, jnp.concatenate([tx, tg], axis=1)).astype(jnp.bfloat16)
            for j in range(TILES):
                part = both[j * SUB : (j + 1) * SUB]
                rows[c, dp, g * SUB : (g + 1) * SUB, j * LANE : (j + 1) * LANE] = part[:, :LANE]
                rows[c, dp, g * SUB : (g + 1) * SUB, (TILES + j) * LANE : (TILES + j + 1) * LANE] = part[:, LANE:]
        mine = rows.at[c, dp]
        send(mine, mine, a_send.at[c], y_recv.at[c, 0], up)
        send(mine, mine, a_send.at[c], y_recv.at[c, 1], down)
        send(mine, mine, a_send.at[c], c_recv.at[c, 0], twin)

    def forward(c):
        low, high = pl.ds(0, SUB), pl.ds(SUB, SUB)
        take(rows.at[c, d_down], y_recv.at[c, 0])
        block = rows.at[c, d_down, low]
        send(block, block, f_send.at[c], y_recv.at[c, 2], up)
        take(rows.at[c, d_up], y_recv.at[c, 1])
        block = rows.at[c, d_up, high]
        send(block, block, f_send.at[c], y_recv.at[c, 3], down)
        send(rows.at[c, d_down], rows.at[c, d_down], f_send.at[c], c_recv.at[c, 1], twin)
        send(rows.at[c, d_up], rows.at[c, d_up], f_send.at[c], c_recv.at[c, 2], twin)

    def forward_far(c):
        for i in range(2):
            block = rows.at[c, d_far, pl.ds(i * SUB, SUB)]
            take(block, y_recv.at[c, 2 + i])
            send(block, block, h_send.at[c], c_recv.at[c, 3], twin)

    def hidden(c, f):
        at = pl.ds(f * 256, 256)
        x_rows = rows[c, :, :, :feat].reshape(2 * NY * 32, feat)
        g_rows = rows[c, :, :, feat:].reshape(2 * NY * 32, feat)
        value, slope = gelu_parts(dot_nt(w_in[at, :], x_rows))
        pre_grad = (dot_nt(w_out[at, :], g_rows) * slope).astype(jnp.bfloat16)
        act_t[c, at] = value.astype(jnp.bfloat16)
        pg_t[c, at] = pre_grad
        pre_grad = pre_grad.T
        pre_grad = pre_grad.reshape(NY, 2, 32, 256)
        for core in range(2):
            pg[(core + k) % 2, :, :, at] = pre_grad[:, core]

    def hidden_low(c):
        t_own, t_down = y * 2 + 1 - k, y_down * 2 + 1 - k
        t_up, t_far = y_up * 2 + 1 - k, y_far * 2 + 1 - k
        for i, d in enumerate((t_own, t_down, t_up, t_far)):
            take(rows.at[c, d], c_recv.at[c, i])
        hidden(c, 0)

    def hidden_high(c):
        hidden(c, 1)

    def rows_grad(c):
        def part_of(f, _):
            at = pl.ds(pl.multiple_of(f * 512, 512), 512)
            part = dot_nn(pg[...].reshape(2 * NY * 32, hid), w_in[:, at]).reshape(2, NY, 32, 512)
            own[c % 4, :, :, at] = part[0]
            tsend[c, :, :, at] = part[1].astype(jnp.bfloat16)
            return 0

        lax.fori_loop(0, feat // 512, part_of, 0)
        send(tsend.at[c], trecv.at[c], t_send.at[c], t_recv.at[c], twin)

    def reduce_far(c):
        take(trecv.at[c], t_recv.at[c])
        o = c % 4
        for i in range(2):
            at = pl.ds(i * SUB, SUB)
            r1s[c, i] = (own[o, y_far, at] + trecv[c, y_far, at].astype(jnp.float32)).astype(jnp.bfloat16)
        send(r1s.at[c, 0], r1r.at[c, 0], r1_send.at[c], r1_recv.at[c, 0], up)
        send(r1s.at[c, 1], r1r.at[c, 1], r1_send.at[c], r1_recv.at[c, 1], down)

    def reduce_near(c):
        o = c % 4
        for i, (to, y_to, first) in enumerate(((up, y_up, 0), (down, y_down, SUB))):
            take(r1r.at[c, i], r1_recv.at[c, i])
            with_far, alone = pl.ds(first, SUB), pl.ds(SUB - first, SUB)
            total = own[o, y_to, with_far] + trecv[c, y_to, with_far].astype(jnp.float32)
            r2s[c, i, with_far] = (total + r1r[c, i].astype(jnp.float32)).astype(jnp.bfloat16)
            total = own[o, y_to, alone] + trecv[c, y_to, alone].astype(jnp.float32)
            r2s[c, i, alone] = total.astype(jnp.bfloat16)
            send(r2s.at[c, i], r2r.at[c, i], r2_send.at[c], r2_recv.at[c, i], to)
        own_sum = own[o, y] + trecv[c, y].astype(jnp.float32)
        own[o, y] = own_sum

    def reduce_last(c):
        o = c % 4
        for i in range(2):
            take(r2r.at[c, i], r2_recv.at[c, i])
        for g in range(2):
            at = pl.ds(g * SUB, SUB)
            total = own[o, y, at] + r2r[c, 0, at].astype(jnp.float32) + r2r[c, 1, at].astype(jnp.float32)
            total = total.astype(jnp.bfloat16)
            out = dot_nn(swap, to_tiles(total, TILES)).astype(jnp.bfloat16)
            fin[c, g * SUB : (g + 1) * SUB] = out.reshape(SUB, TILES, LANE)
        exchange(c, fin, back, b_send, b_recv, -1)

    def finish(c):
        take(back.at[c], b_recv.at[c])
        tall = jnp.concatenate([back[c, g * SUB : (g + 1) * SUB].reshape(SUB * TILES, LANE) for g in range(2)], axis=1)
        flat = dot_nn(swap, tall).astype(jnp.bfloat16)
        for g in range(2):
            for j in range(TILES):
                at = slice(g * LANE, (g + 1) * LANE)
                slots[c, g * SUB : (g + 1) * SUB, j * LANE : (j + 1) * LANE] = flat[j * SUB : (j + 1) * SUB, at]

        @pl.when(c == CAP - 1)
        def _():
            def combine(f, _):
                at = pl.ds(pl.multiple_of(f * 512, 512), 512)
                grad = lax.dot_general(
                    place[...].reshape(CAP * n_hold, LANE), slots[:, :, at].reshape(CAP * n_hold, 512),
                    (((0,), (0,)), ((), ())), preferred_element_type=jnp.float32,
                )
                grad_ref[:, at] = grad.astype(jnp.bfloat16)
                return 0

            lax.fori_loop(0, feat // 512, combine, 0)

    def weight_grads(f):
        at = pl.ds(pl.multiple_of(f * 256, 256), 256)
        at_g = pl.ds(pl.multiple_of(feat + f * 256, 256), 256)
        total_in = total_out = None
        for c in range(CAP):
            part_in = dot_nn(pg_t[c], rows[c, :, :, at].reshape(2 * NY * 32, 256))
            part_out = dot_nn(act_t[c], rows[c, :, :, at_g].reshape(2 * NY * 32, 256))
            total_in = part_in if c == 0 else total_in + part_in
            total_out = part_out if c == 0 else total_out + part_out
        gw_in_ref[:, at] = total_in.astype(jnp.bfloat16)
        gw_out_ref[:, at] = total_out.astype(jnp.bfloat16)

    dispatch(0)
    pl.semaphore_wait(barrier, n_hold - 1 + 3)
    start_exchange(0)
    dispatch(1)
    dispatch(2)

    def outputs_even(c):
        weight_grads(2 * c)

    def outputs_odd(c):
        weight_grads(2 * c + 1)

    stages = [
        (1, CAP, forward),
        (0, CAP, start_gather),
        (2, CAP, hidden_low),
        (1, CAP, forward_far),
        (2, CAP, hidden_high),
        (3, CAP, reduce_far),
        (2, CAP, rows_grad),
        (4, CAP, reduce_near),
        (0, CAP, prepare),
        (7, 4, outputs_even),
        (5, CAP, reduce_last),
        (7, 4, outputs_odd),
        (6, CAP, finish),
    ]

    def tick(t, _):
        @pl.when(t == 2)
        def _():
            for copy in w_copies:
                copy.wait()

        for first, count, stage in stages:
            pl.when((t >= first) & (t < first + count))(functools.partial(stage, t - first))

        return 0

    lax.fori_loop(0, 11, tick, 0)

    def drain(c, _):
        sent(c, in_tiles, e_send)
        take(rows.at[c, pl.ds(0, 3)], a_send.at[c])
        take(rows.at[c, pl.ds(0, 3)], f_send.at[c])
        take(rows.at[c, 0], h_send.at[c])
        take(tsend.at[c], t_send.at[c])
        take(r1s.at[c], r1_send.at[c])
        take(r2s.at[c], r2_send.at[c])
        sent(c, fin, b_send)
        return 0

    lax.fori_loop(0, CAP, drain, 0)


def write_out(grad_v, gw_in_v, gw_out_v, grad_h, gw_in_h, gw_out_h, sem):
    rows = grad_v.shape[0]
    parts = [(grad_v, grad_h, 0)]
    for first in range(0, gw_in_v.shape[0], rows):
        parts += [(gw_in_v, gw_in_h, first), (gw_out_v, gw_out_h, first)]
    copies = [
        pltpu.make_async_copy(src.at[pl.ds(first, rows)], dst.at[pl.ds(first, rows)], sem.at[i])
        for i, (src, dst, first) in enumerate(parts)
    ]
    for copy in copies:
        copy.start()
    for copy in copies:
        copy.wait()


def exchange_and_compute(route, both, w_first, w_second):
    hid, feat = w_first.shape
    bf16, f32 = jnp.bfloat16, jnp.float32
    n_hold = NX * NZ
    vmem, anywhere = pl.BlockSpec(memory_space=pltpu.VMEM), pl.BlockSpec(memory_space=pl.ANY)
    hbm = pl.BlockSpec(memory_space=pltpu.HBM)
    dma = pltpu.SemaphoreType.DMA
    shapes = (
        jax.ShapeDtypeStruct((both.shape[0], feat), bf16),
        jax.ShapeDtypeStruct((hid, feat), bf16),
        jax.ShapeDtypeStruct((hid, feat), bf16),
    )
    made = pl.pallas_call(
        kernel,
        out_shape=shapes,
        in_specs=[vmem, vmem, hbm, hbm],
        out_specs=(vmem, vmem, vmem),
        scratch_shapes=[
            pltpu.VMEM((hid, feat), bf16),
            pltpu.VMEM((hid, feat), bf16),
            pltpu.VMEM((CAP, n_hold, 128), bf16),
            pltpu.VMEM((CAP, n_hold, 2 * TILES, LANE), bf16),
            pltpu.VMEM((CAP, n_hold, 2 * TILES, LANE), bf16),
            pltpu.VMEM((CAP, 2 * NY, 32, 2 * feat), bf16),
            pltpu.VMEM((CAP, hid, 256), bf16),
            pltpu.VMEM((CAP, hid, 256), bf16),
            pltpu.VMEM((2, NY, 32, hid), bf16),
            pltpu.VMEM((CAP, n_hold, feat), bf16),
            pltpu.VMEM((CAP, NY, 32, feat), bf16),
            pltpu.VMEM((CAP, NY, 32, feat), bf16),
            pltpu.VMEM((4, NY, 32, feat), f32),
            pltpu.VMEM((CAP, 2, SUB, feat), bf16),
            pltpu.VMEM((CAP, 2, SUB, feat), bf16),
            pltpu.VMEM((CAP, 2, 32, feat), bf16),
            pltpu.VMEM((CAP, 2, 32, feat), bf16),
            pltpu.VMEM((CAP, n_hold, TILES, LANE), bf16),
            pltpu.VMEM((CAP, n_hold, TILES, LANE), bf16),
            dma((2,)),
            dma((CAP,)), dma((CAP,)),
            dma((CAP,)), dma((CAP,)), dma((CAP,)),
            dma((CAP, 4)), dma((CAP, 4)),
            dma((CAP,)), dma((CAP,)),
            dma((CAP,)), dma((CAP, 2)),
            dma((CAP,)), dma((CAP, 2)),
            dma((CAP,)), dma((CAP,)),
        ],
        compiler_params=pltpu.CompilerParams(
            collective_id=0, has_side_effects=True, vmem_limit_bytes=48 * 1024 * 1024
        ),
    )(route, both, w_first, w_second)
    return pl.pallas_call(
        write_out,
        out_shape=shapes,
        in_specs=[vmem] * 3,
        out_specs=(anywhere,) * 3,
        scratch_shapes=[dma((1 + 2 * hid // both.shape[0],))],
        compiler_params=pltpu.CompilerParams(vmem_limit_bytes=1024 * 1024),
    )(*made)


def body(inputs, grad_out, lang_ids, lang_block, block_owner, w_in, w_out):
    lang_row = jnp.pad(lang_block, (0, 256 - lang_block.shape[0]), constant_values=-1)
    owner_row = jnp.pad(block_owner, (0, 128 - block_owner.shape[0]), constant_values=-1)
    route = jnp.concatenate([lang_row, owner_row, lang_ids])[None]
    grad_in, g_in, g_out = exchange_and_compute(route, jnp.concatenate([inputs, grad_out], axis=1), w_in[0], w_out[0])
    return (grad_in, g_in[None], g_out[None])


def solution(mesh):
    in_specs = (
        P(("dp", "lang"), None),
        P(("dp", "lang"), None),
        P(("dp", "lang")),
        P(),
        P(),
        P("lang", "dp", None),
        P("lang", "dp", None),
    )
    out_specs = (P(("dp", "lang"), None), P("lang", "dp", None), P("lang", "dp", None))
    return jax.shard_map(body, mesh=mesh, in_specs=in_specs, out_specs=out_specs, check_vma=False)
```
